32 devices in a mesh: groups: 2 (over y), dp: 4 (over z), mp: 2 (over x), layer: 2 (over core).
Axes of the slice: x: 2, y: 2, z: 4, core: 2. Of those that a mesh axis runs over, the one named last changes fastest.
Arguments:
- acts: bfloat16 [2, 4096, 8192], P('layer', ('groups', 'dp'), 'mp'), parts along dimension 1, may hold values from -6 to 6
- grads: bfloat16 [2, 4096, 28672], P('layer', ('groups', 'dp'), 'mp'), parts along dimension 1, may hold values from -6 to 6
- query_left: bfloat16 [2, 8192, 512], P('layer', ('mp', 'dp'), 'groups'), parts along dimension 2, may hold values from -0.0625 to 0.0625
- query_right: bfloat16 [2, 28672, 512], P('layer', ('mp', 'dp'), 'groups'), parts along dimension 2, may hold values from -0.03125 to 0.03125
- seq_len: int32 [16], P(('groups', 'dp')), parts along dimension 0, may hold values from 1 to 256, 1024 in all
Outputs:
- scores: float32 [2, 16, 32], P('layer', ('groups', 'dp')), parts along dimension 1
The draws below stay inside these ranges and needn't reach their ends.
There are 2 independent parts, one for each index of `groups`. The reference program is written for one: setup_inputs(seed, part) draws one part's arguments, and reference() takes and returns one part's arrays. A program takes and returns all parts, laid end to end along the dimension named above; each array names one. Nothing has to cross between parts.
Inputs may be any that keep to these rules, and one draw needn't show every extreme that they name: `seq_len`: every sequence has at least one live token and some sequence has exactly 256.
All inputs are finite; a program needn't handle non-finite values. No bound on the sum of `seq_len` on one device may be relied on, other than what follows from the above.
Results may differ from the reference program's by a relative error of at most 0.0003.
Values may be sent and summed in bfloat16 or wider, within the bound.
No kernel may reach another device: no remote copies, remote signals or barrier semaphores. Data moves between devices by JAX's collectives and lax.ppermute only.
A program may use at most 64 MiB of HBM per device.

```python
import math
import jax
import jax.numpy as jnp
import numpy as np
from jax import lax

D = 8192
F = 28672
NQ = 32
RANK = 8
LAYERS = 2
LEN = 256
SEQS = 8
TOKENS = 2048
QR = 256


def levels(rng, dims, cuts, low, high):
    def one(axis_at, blocks):
        steps = jax.random.uniform(jax.random.fold_in(jax.random.fold_in(rng, 6), axis_at), (blocks,), jnp.float32, low / len(cuts), high / len(cuts))
        return jnp.repeat(jnp.exp(steps), dims[axis_at] // blocks).reshape((-1,) + (1,) * (len(dims) - axis_at - 1))

    level = one(*cuts[0])
    for cut in cuts[1:]:
        level = level * one(*cut)
    return level


def profile(number_of, total, reach, lean):
    loads = [(1 << 20) // math.isqrt(standing ** lean) + 1 for standing in range(2, number_of + 1)]
    rest, holding = total - reach - (number_of - 1), [1] * (number_of - 1)
    while rest > 0:
        free = [i for i in range(number_of - 1) if holding[i] < reach]
        mass, left = sum([loads[i] for i in free]), rest
        for i in free:
            more = min(reach - holding[i], max(1, left * loads[i] // mass), rest)
            holding[i] = holding[i] + more
            rest = rest - more
    return np.array([reach] + holding)


def uneven(rng, number_of, total, limit, skew):
    if number_of == 2:
        one = jax.random.randint(rng, (), max(1, total - limit), min(limit, total - 1) + 1)
        return jnp.stack([one, total - one])
    tallies = jnp.asarray(profile(number_of, total, limit, skew), jnp.int32)
    twos = (number_of - 1) // 2
    giver, receiver = tallies[1:1 + 2 * twos:2], tallies[2:2 + 2 * twos:2]
    room = jnp.minimum(giver - 1, limit - receiver)
    passed = jax.random.randint(jax.random.fold_in(rng, 1), (twos,), 0, 1 << 20) % (room + 1)
    tallies = tallies.at[1:1 + 2 * twos:2].set(giver - passed).at[2:2 + 2 * twos:2].set(receiver + passed)
    return tallies[jax.random.permutation(jax.random.fold_in(rng, 2), number_of)]


def noise(rng, extent, width, reach, split=(), held_as=jnp.bfloat16):
    gain = levels(rng, extent, split, -0.22, 0.18) if split else 1.0
    entries = jax.random.normal(rng, extent, jnp.float32) * width * gain
    return jnp.minimum(jnp.maximum(entries, -reach), reach).astype(held_as)


def setup_inputs(seed: int = 0, part: int = 0) -> dict:
    arg_keys = jax.random.split(jax.random.key(seed), 6)
    part_splits = jax.random.split(jax.random.fold_in(arg_keys[5], part), 6)
    return {
        "acts": noise(part_splits[0], (LAYERS, TOKENS, D), 1.0, 6.0, ((0, 2), (1, 4), (2, 2))),
        "grads": noise(part_splits[1], (LAYERS, TOKENS, F), 1.0, 6.0, ((0, 2), (1, 4), (2, 2))),
        "query_left": noise(part_splits[2], (LAYERS, D, QR), D ** -0.5, 0.0625, ((0, 2), (1, 8))),
        "query_right": noise(part_splits[3], (LAYERS, F, QR), F ** -0.5, 0.03125, ((0, 2), (1, 8))),
        "seq_len": uneven(part_splits[4], SEQS, SEQS * LEN // 2, LEN, 2).astype(jnp.int32),
    }


def layer_scores(acts_layer, grads_layer, left_layer, right_layer, seq_len):
    proj_acts = jnp.dot(acts_layer, left_layer, preferred_element_type=jnp.float32)
    proj_grads = jnp.dot(grads_layer, right_layer, preferred_element_type=jnp.float32)
    product = (proj_acts * proj_grads).reshape(SEQS, LEN, QR)
    positions = jnp.arange(LEN, dtype=jnp.int32)
    live_mask = (positions[None, :] < seq_len[:, None]).astype(product.dtype)
    summed = lax.optimization_barrier(jnp.sum(product * live_mask[:, :, None], axis=1))
    return lax.optimization_barrier(jnp.sum(summed.reshape(SEQS, NQ, RANK), axis=2)) / math.sqrt(RANK * LEN)

def reference(acts, grads, query_left, query_right, seq_len):
    outputs = []
    for layer_index in range(LAYERS):
        outputs.append(layer_scores(acts[layer_index], grads[layer_index], query_left[layer_index], query_right[layer_index], seq_len))
    return jnp.stack(outputs)
```

```python
import math

import jax
import jax.numpy as jnp
from jax import lax
from jax.sharding import PartitionSpec as P

RANK = 8
LEN = 256

TO_END = [(1, 0), (2, 3)]
ACROSS = [(1, 2), (2, 1)]
TO_MIDDLE = [(0, 1), (3, 2)]


def live_rows(seq_len, row_count):
    seq_count = seq_len.shape[0]
    seq_span = row_count // seq_count
    positions = lax.broadcasted_iota(jnp.int32, (seq_count, seq_span, 1), 1)
    live = (positions < seq_len[:, None, None]).astype(jnp.float32)
    return live.reshape(row_count, 1)


def column_scores(masked_acts, proj_grads, seq_count):
    product = masked_acts * proj_grads
    return jnp.sum(product.reshape(seq_count, -1, product.shape[1]), axis=1)


def finish(columns):
    seq_count = columns.shape[0]
    scores = jnp.sum(columns.reshape(seq_count, -1, RANK), axis=2)
    return lax.psum(scores, "mp") / math.sqrt(RANK * LEN)


def dot(a, b):
    return jnp.dot(a, b, preferred_element_type=jnp.float32)


def on_any(acts, grads, left, right, seq_len):
    seq_count = seq_len.shape[0]
    live = live_rows(seq_len, acts.shape[0])
    proj_acts = dot(acts, lax.all_gather(left, "dp", axis=0, tiled=True))
    proj_grads = dot(grads, lax.all_gather(right, "dp", axis=0, tiled=True))
    masked = lax.psum(proj_acts, "mp") * live
    return finish(column_scores(masked, proj_grads, seq_count))


def on_line(acts, grads, left, right, seq_len):
    seq_count = seq_len.shape[0]
    row_count = acts.shape[0]
    place = lax.axis_index("dp")
    is_end = (place == 0) | (place == 3)
    near = place ^ 1
    far_middle = jnp.where(place < 2, 2, 1)
    far_end = jnp.where(place < 2, 3, 0)

    depth = right.shape[0]
    kept = depth * 2 // 7
    piece = (depth - kept) // 2
    cuts = [(0, kept), (kept, kept + piece), (kept + piece, depth)]
    chunks = [left] + [right[a:b] for a, b in cuts]

    to_end = lambda x: lax.ppermute(x, "dp", TO_END)
    across = lambda x: lax.ppermute(x, "dp", ACROSS)
    to_middle = lambda x: lax.ppermute(x, "dp", TO_MIDDLE)

    own, near_in, middle_in, end_in = chunks, [], [], []
    for index, chunk in enumerate(chunks):
        from_end = to_middle(chunk)
        from_middle = across(chunk)
        from_far = across(from_end)
        if index < 2:
            near_in.append(jnp.where(is_end, to_end(chunk), from_end))
        else:
            near_in.append(from_end)
        middle_in.append(jnp.where(is_end, to_end(from_middle), from_middle))
        end_in.append(jnp.where(is_end, to_end(from_far), from_far))

    sources = [(place, own), (near, near_in), (far_middle, middle_in), (far_end, end_in)]

    def columns(array, source, span, start, stop):
        return lax.dynamic_slice_in_dim(array, source * span + start, stop - start, axis=1)

    proj_acts = sum(
        dot(columns(acts, source, left.shape[0], 0, left.shape[0]), got[0])
        for source, got in sources
    )
    masked = lax.psum(proj_acts, "mp") * live_rows(seq_len, row_count)

    proj_grads = None
    for index, (start, stop) in enumerate(cuts):
        for source, got in sources:
            term = dot(columns(grads, source, depth, start, stop), got[index + 1])
            proj_grads = term if proj_grads is None else proj_grads + term

    guest_acts = to_middle(masked)
    guest_grads = None
    for start, stop in cuts[1:]:
        guest = to_middle(columns(grads, near, depth, start, stop))
        term = dot(guest, right[start:stop])
        guest_grads = term if guest_grads is None else guest_grads + term
    guest_scores = to_end(column_scores(guest_acts, guest_grads, seq_count))

    return finish(column_scores(masked, proj_grads, seq_count) + guest_scores)


def solution(mesh):
    body = on_line if mesh.shape["dp"] == 4 else on_any

    def on_device(acts, grads, query_left, query_right, seq_len):
        return body(acts[0], grads[0], query_left[0], query_right[0], seq_len)[None]

    return jax.shard_map(
        on_device,
        mesh=mesh,
        in_specs=(
            P("layer", ("groups", "dp"), "mp"),
            P("layer", ("groups", "dp"), "mp"),
            P("layer", ("mp", "dp"), "groups"),
            P("layer", ("mp", "dp"), "groups"),
            P(("groups", "dp")),
        ),
        out_specs=P("layer", ("groups", "dp"), None),
        check_vma=False,
    )
```

```python
import math

import jax
import jax.numpy as jnp
from jax import lax
from jax.sharding import PartitionSpec as P

RANK = 8
LEN = 256

TRADE = [(0, 1), (1, 0), (2, 3), (3, 2)]
TO_END = [(1, 0), (2, 3)]
ACROSS = [(1, 2), (2, 1)]
TO_MIDDLE = [(0, 1), (3, 2)]


def live_rows(seq_len, row_count):
    seq_count = seq_len.shape[0]
    seq_span = row_count // seq_count
    positions = lax.broadcasted_iota(jnp.int32, (seq_count, seq_span, 1), 1)
    live = (positions < seq_len[:, None, None]).astype(jnp.float32)
    return live.reshape(row_count, 1)


def column_scores(masked_acts, proj_grads, seq_count):
    product = masked_acts * proj_grads
    return jnp.sum(product.reshape(seq_count, -1, product.shape[1]), axis=1)


def finish(columns):
    seq_count = columns.shape[0]
    scores = jnp.sum(columns.reshape(seq_count, -1, RANK), axis=2)
    return lax.psum(scores, "mp") / math.sqrt(RANK * LEN)


def dot(a, b):
    return jnp.dot(a, b, preferred_element_type=jnp.float32)


def on_any(acts, grads, left, right, seq_len):
    seq_count = seq_len.shape[0]
    live = live_rows(seq_len, acts.shape[0])
    proj_acts = dot(acts, lax.all_gather(left, "dp", axis=0, tiled=True))
    proj_grads = dot(grads, lax.all_gather(right, "dp", axis=0, tiled=True))
    masked = lax.psum(proj_acts, "mp") * live
    return finish(column_scores(masked, proj_grads, seq_count))


def on_line(acts, grads, left, right, seq_len):
    seq_count = seq_len.shape[0]
    row_count = acts.shape[0]
    place = lax.axis_index("dp")
    is_end = (place == 0) | (place == 3)
    near = place ^ 1
    far_middle = jnp.where(place < 2, 2, 1)
    far_end = jnp.where(place < 2, 3, 0)

    unit = left.shape[0]
    depth = right.shape[0]
    half = unit // 2
    spans = {"B": (0, unit), "C1": (unit, 2 * unit), "C2": (2 * unit, 3 * unit), "C3": (3 * unit, depth)}
    own = {"A": left}
    own.update({name: right[start:stop] for name, (start, stop) in spans.items()})

    trade = sender(TRADE)
    across = sender(ACROSS)
    to_end = lambda x: lax.ppermute(x, "dp", TO_END)
    to_middle = lambda x: lax.ppermute(x, "dp", TO_MIDDLE)

    def columns(array, source, start, stop):
        span = array.shape[1] // 4
        return lax.dynamic_slice_in_dim(array, source * span + start, stop - start, axis=1)

    def guest(index):
        block = columns(grads, near, unit + index * half, unit + (index + 1) * half)
        return jnp.concatenate([block[:, : half // 2], block[:, half // 2 :]], axis=0)

    def either(at_end, at_middle):
        return jnp.where(is_end, at_end, at_middle)

    x, y = {}, {}
    x["A"] = trade(own["A"])
    y["AM"] = across(own["A"])
    x["B"] = trade(own["B"])
    y["BM"] = across(own["B"])
    y["AE"] = across(x["A"])
    x["AM"] = trade(either(own["C1"], y["AM"]))
    y["C1M"] = across(own["C1"])
    x["BM"] = trade(either(own["C2"], y["BM"]))
    y["C2M"] = across(own["C2"])
    x["AE"] = trade(either(guest(0), y["AE"]))
    y["C3M"] = across(own["C3"])
    x["C1M"] = trade(either(guest(1), y["C1M"]))
    y["BE"] = across(x["B"])
    x["C2M"] = trade(either(guest(2), y["C2M"]))
    y["C1E"] = across(x["AM"])
    x["C3M"] = trade(either(own["C3"], y["C3M"]))
    y["C2E"] = across(x["BM"])
    x["BE"] = trade(either(guest(3), y["BE"]))
    y["C3E"] = across(x["C3M"])
    x["C1E"] = trade(either(guest(4), y["C1E"]))
    x["C2E"] = trade(y["C2E"], TO_END)
    x["C3E"] = trade(y["C3E"], TO_END)

    proj_acts = (
        dot(columns(acts, place, 0, unit), own["A"])
        + dot(columns(acts, near, 0, unit), x["A"])
        + dot(columns(acts, far_middle, 0, unit), either(x["AM"], y["AM"]))
        + dot(columns(acts, far_end, 0, unit), either(x["AE"], y["AE"]))
    )
    other_acts = lax.ppermute(proj_acts, "mp", [(0, 1), (1, 0)])
    masked = (proj_acts + other_acts) * live_rows(seq_len, row_count)

    proj_grads = dot(columns(grads, place, 0, depth), right)
    proj_grads += dot(columns(grads, near, *spans["B"]), x["B"])
    for name, holder in (("C1", "AM"), ("C2", "BM"), ("C3", "C3M")):
        proj_grads += dot(columns(grads, near, *spans[name]), either(jnp.zeros_like(x[holder]), x[holder]))
    for name in ("B", "C1", "C2", "C3"):
        proj_grads += dot(columns(grads, far_middle, *spans[name]), either(x[name + "M"], y[name + "M"]))
    for name in ("B", "C1", "C2", "C3"):
        proj_grads += dot(columns(grads, far_end, *spans[name]), either(x[name + "E"], y[name + "E"]))

    guest_acts = to_middle(masked)
    guest_grads = 0.0
    for index, name in enumerate(("AE", "C1M", "C2M", "BE", "C1E")):
        start = unit + index * half
        for block in (0, 1):
            rows = x[name][block * row_count : (block + 1) * row_count]
            begin = start + block * (half // 2)
            guest_grads += dot(rows, right[begin : begin + half // 2])
    guest_scores = to_end(column_scores(guest_acts, guest_grads, seq_count))

    return finish(column_scores(masked, proj_grads, seq_count) + guest_scores)


def sender(pairs):
    came = []

    def send(x, pairs=pairs):
        if len(came) >= 2:
            x, came[-2] = lax.optimization_barrier((x, came[-2]))
        came.append(lax.ppermute(x, "dp", pairs))
        return came[-1]

    return send


def suits_line(mesh, acts, left, right):
    unit = left.shape[0]
    fits = right.shape[0] * 2 == unit * 7 and acts.shape[0] * 2 == unit and left.shape[1] * 4 == unit
    return mesh.shape["dp"] == 4 and mesh.shape["mp"] == 2 and fits


def solution(mesh):
    def on_device(acts, grads, query_left, query_right, seq_len):
        body = on_line if suits_line(mesh, acts[0], query_left[0], query_right[0]) else on_any
        return body(acts[0], grads[0], query_left[0], query_right[0], seq_len)[None]

    return jax.shard_map(
        on_device,
        mesh=mesh,
        in_specs=(
            P("layer", ("groups", "dp"), "mp"),
            P("layer", ("groups", "dp"), "mp"),
            P("layer", ("mp", "dp"), "groups"),
            P("layer", ("mp", "dp"), "groups"),
            P(("groups", "dp")),
        ),
        out_specs=P("layer", ("groups", "dp"), None),
        check_vma=False,
    )
```

```python
import math

import jax
import jax.numpy as jnp
from jax import lax
from jax.sharding import PartitionSpec as P

RANK = 8
LEN = 256

TRADE = [(0, 1), (1, 0), (2, 3), (3, 2)]
TO_END = [(1, 0), (2, 3)]
ACROSS = [(1, 2), (2, 1)]
TO_MIDDLE = [(0, 1), (3, 2)]


def live_rows(seq_len, row_count):
    seq_count = seq_len.shape[0]
    seq_span = row_count // seq_count
    positions = lax.broadcasted_iota(jnp.int32, (seq_count, seq_span, 1), 1)
    live = (positions < seq_len[:, None, None]).astype(jnp.float32)
    return live.reshape(row_count, 1)


def column_scores(masked_acts, proj_grads, seq_count):
    product = masked_acts * proj_grads
    return jnp.sum(product.reshape(seq_count, -1, product.shape[1]), axis=1)


def rank_scores(columns):
    seq_count = columns.shape[0]
    return jnp.sum(columns.reshape(seq_count, -1, RANK), axis=2)


def dot(a, b):
    return jnp.dot(a, b, preferred_element_type=jnp.float32)


def on_any(acts, grads, left, right, seq_len):
    seq_count = seq_len.shape[0]
    live = live_rows(seq_len, acts.shape[0])
    proj_acts = dot(acts, lax.all_gather(left, "dp", axis=0, tiled=True))
    proj_grads = dot(grads, lax.all_gather(right, "dp", axis=0, tiled=True))
    masked = lax.psum(proj_acts, "mp") * live
    scores = rank_scores(column_scores(masked, proj_grads, seq_count))
    return lax.psum(scores, "mp") / math.sqrt(RANK * LEN)


def after(value, *arrived):
    return lax.optimization_barrier((value, *arrived))[0]


class Sender:
    def __init__(self, pairs):
        self.pairs = pairs
        self.came = []

    def ready(self, value, *arrived):
        return after(value, *self.came[-2:-1], *arrived)

    def __call__(self, x, pairs=None):
        self.came.append(lax.ppermute(x, "dp", pairs or self.pairs))
        return self.came[-1]


def on_line(acts, grads, left, right, seq_len):
    seq_count = seq_len.shape[0]
    row_count = acts.shape[0]
    place = lax.axis_index("dp")
    is_end = (place == 0) | (place == 3)
    near = place ^ 1
    far_middle = jnp.where(place < 2, 2, 1)
    far_end = jnp.where(place < 2, 3, 0)

    unit = left.shape[0]
    depth = right.shape[0]
    half = unit // 2
    spans = {"B": (0, unit), "C1": (unit, 2 * unit), "C2": (2 * unit, 3 * unit), "C3": (3 * unit, depth)}
    trade = Sender(TRADE)
    across = Sender(ACROSS)

    def columns(array, source, start, stop):
        span = array.shape[1] // 4
        return lax.dynamic_slice_in_dim(array, source * span + start, stop - start, axis=1)

    def own(name, sender):
        start, stop = spans[name]
        return sender.ready(right)[start:stop]

    def guest(index, sender):
        source = sender.ready(grads)
        start = unit + index * half
        middle = start + half // 2
        blocks = [columns(source, near, start, middle), columns(source, near, middle, start + half)]
        return jnp.concatenate(blocks, axis=0)

    def either(at_end, at_middle):
        return jnp.where(is_end, at_end, at_middle)

    x, y = {}, {}
    x["A"] = trade(left)
    y["AM"] = across(left)
    first = right[:unit]
    x["B"] = trade(first)
    y["BM"] = across(first)
    y["AE"] = across(across.ready(x["A"]))
    x["AM"] = trade(either(own("C1", trade), y["AM"]))
    y["C1M"] = across(own("C1", across))
    x["BM"] = trade(either(own("C2", trade), y["BM"]))
    y["C2M"] = across(own("C2", across))
    x["AE"] = trade(either(guest(0, trade), y["AE"]))
    y["C3M"] = across(own("C3", across))
    x["C1M"] = trade(either(guest(1, trade), y["C1M"]))
    y["BE"] = across(across.ready(x["B"]))
    x["C2M"] = trade(either(guest(2, trade), y["C2M"]))
    y["C1E"] = across(across.ready(x["AM"]))
    x["C3M"] = trade(either(own("C3", trade), y["C3M"]))
    y["C2E"] = across(across.ready(x["BM"]))
    x["BE"] = trade(either(guest(3, trade), y["BE"]))
    y["C3E"] = across(across.ready(x["C3M"], x["BE"]))
    x["C1E"] = trade(either(guest(4, trade), y["C1E"]))
    x["C2E"] = trade(trade.ready(y["C2E"]), TO_END)
    x["C3E"] = trade(trade.ready(y["C3E"]), TO_END)

    proj_acts = dot(columns(after(acts, x["A"], y["AM"]), place, 0, unit), left)
    proj_acts += dot(columns(acts, near, 0, unit), x["A"])
    proj_acts += dot(columns(acts, far_middle, 0, unit), either(x["AM"], y["AM"]))
    proj_acts += dot(columns(acts, far_end, 0, unit), either(x["AE"], y["AE"]))
    other_acts = lax.ppermute(proj_acts, "mp", [(0, 1), (1, 0)])
    masked = after((proj_acts + other_acts) * live_rows(seq_len, row_count))
    guest_acts = lax.ppermute(masked, "dp", TO_MIDDLE)

    def near_term(name, got):
        if name != "B":
            got = either(jnp.zeros_like(got), got)
        return dot(columns(grads, near, *spans[name]), got)

    def middle_term(name):
        return dot(columns(grads, far_middle, *spans[name]), either(x[name + "M"], y[name + "M"]))

    def end_term(name):
        return dot(columns(grads, far_end, *spans[name]), either(x[name + "E"], y[name + "E"]))

    def guest_term(index, got):
        start = unit + index * half
        terms = []
        for block in (0, 1):
            rows = got[block * row_count : (block + 1) * row_count]
            begin = start + block * (half // 2)
            terms.append(dot(rows, right[begin : begin + half // 2]))
        return terms[0] + terms[1]

    proj_grads = dot(columns(after(grads, x["B"], y["BM"]), place, 0, depth), right)
    proj_grads += near_term("B", x["B"])
    proj_grads = after(proj_grads)
    proj_grads += near_term("C1", x["AM"])
    proj_grads += middle_term("B")
    proj_grads += near_term("C2", x["BM"])
    proj_grads = after(proj_grads)
    guest_grads = guest_term(0, x["AE"])
    proj_grads += middle_term("C1")
    guest_grads += guest_term(1, x["C1M"])
    proj_grads, guest_grads = lax.optimization_barrier((proj_grads, guest_grads))
    proj_grads += middle_term("C2")
    guest_grads += guest_term(2, x["C2M"])
    proj_grads += middle_term("C3")
    proj_grads += near_term("C3", x["C3M"])
    proj_grads, guest_grads, masked = lax.optimization_barrier((proj_grads, guest_grads, masked))
    proj_grads += end_term("B")
    guest_grads += guest_term(3, x["BE"])
    proj_grads, guest_grads = lax.optimization_barrier((proj_grads, guest_grads))
    proj_grads += end_term("C1")
    guest_grads += guest_term(4, x["C1E"])
    guest_scores = lax.ppermute(column_scores(guest_acts, guest_grads, seq_count), "dp", TO_END)

    proj_grads = after(proj_grads)
    proj_grads = after(proj_grads + end_term("C2"), guest_scores)
    proj_grads += end_term("C3")
    scores = rank_scores(column_scores(masked, proj_grads, seq_count) + guest_scores)
    other_scores = lax.ppermute(scores, "mp", [(0, 1), (1, 0)])
    return (scores + other_scores) / math.sqrt(RANK * LEN)


def suits_line(mesh, acts, left, right):
    unit = left.shape[0]
    fits = right.shape[0] * 2 == unit * 7 and acts.shape[0] * 2 == unit and left.shape[1] * 4 == unit
    return mesh.shape["dp"] == 4 and mesh.shape["mp"] == 2 and fits


def solution(mesh):
    def on_device(acts, grads, query_left, query_right, seq_len):
        body = on_line if suits_line(mesh, acts[0], query_left[0], query_right[0]) else on_any
        return body(acts[0], grads[0], query_left[0], query_right[0], seq_len)[None]

    return jax.shard_map(
        on_device,
        mesh=mesh,
        in_specs=(
            P("layer", ("groups", "dp"), "mp"),
            P("layer", ("groups", "dp"), "mp"),
            P("layer", ("mp", "dp"), "groups"),
            P("layer", ("mp", "dp"), "groups"),
            P(("groups", "dp")),
        ),
        out_specs=P("layer", ("groups", "dp"), None),
        check_vma=False,
    )
```

```python
import math

import jax
import jax.numpy as jnp
from jax import lax
from jax.sharding import PartitionSpec as P

RANK = 8
LEN = 256

TRADE = [(0, 1), (1, 0), (2, 3), (3, 2)]
TO_END = [(1, 0), (2, 3)]
ACROSS = [(1, 2), (2, 1)]
TO_MIDDLE = [(0, 1), (3, 2)]


def live_rows(seq_len, row_count):
    seq_count = seq_len.shape[0]
    seq_span = row_count // seq_count
    positions = lax.broadcasted_iota(jnp.int32, (seq_count, seq_span, 1), 1)
    live = (positions < seq_len[:, None, None]).astype(jnp.float32)
    return live.reshape(row_count, 1)


def column_scores(masked_acts, proj_grads, seq_count):
    product = masked_acts * proj_grads
    return jnp.sum(product.reshape(seq_count, -1, product.shape[1]), axis=1)


def rank_scores(columns):
    seq_count = columns.shape[0]
    return jnp.sum(columns.reshape(seq_count, -1, RANK), axis=2)


def dot(a, b):
    return jnp.dot(a, b, preferred_element_type=jnp.float32)


def on_any(acts, grads, left, right, seq_len):
    seq_count = seq_len.shape[0]
    live = live_rows(seq_len, acts.shape[0])
    proj_acts = dot(acts, lax.all_gather(left, "dp", axis=0, tiled=True))
    proj_grads = dot(grads, lax.all_gather(right, "dp", axis=0, tiled=True))
    masked = lax.psum(proj_acts, "mp") * live
    scores = rank_scores(column_scores(masked, proj_grads, seq_count))
    return lax.psum(scores, "mp") / math.sqrt(RANK * LEN)


def after(value, *arrived):
    return lax.optimization_barrier((value, *arrived))[0]


class Sender:
    def __init__(self, pairs):
        self.pairs = pairs
        self.came = []

    def ready(self, value, *arrived):
        return after(value, *self.came[-2:-1], *arrived)

    def __call__(self, x, pairs=None):
        self.came.append(lax.ppermute(x, "dp", pairs or self.pairs))
        return self.came[-1]


def on_line(acts, grads, left, right, seq_len):
    seq_count = seq_len.shape[0]
    row_count = acts.shape[0]
    place = lax.axis_index("dp")
    is_end = (place == 0) | (place == 3)
    near = place ^ 1
    far_middle = jnp.where(place < 2, 2, 1)
    far_end = jnp.where(place < 2, 3, 0)

    unit = left.shape[0]
    depth = right.shape[0]
    half = unit // 2
    spans = {"B": (0, unit), "C1": (unit, 2 * unit), "C2": (2 * unit, 3 * unit), "C3": (3 * unit, depth)}
    trade = Sender(TRADE)
    across = Sender(ACROSS)

    def columns(array, source, start, stop):
        span = array.shape[1] // 4
        return lax.dynamic_slice_in_dim(array, source * span + start, stop - start, axis=1)

    def own(name, sender):
        start, stop = spans[name]
        return sender.ready(right)[start:stop]

    def guest(index, sender):
        source = sender.ready(grads)
        start = unit + index * half
        middle = start + half // 2
        blocks = [columns(source, near, start, middle), columns(source, near, middle, start + half)]
        return jnp.concatenate(blocks, axis=0)

    def either(at_end, at_middle):
        return jnp.where(is_end, at_end, at_middle)

    x, y = {}, {}
    x["A"] = trade(left)
    y["AM"] = across(left)
    x["B"] = trade(right[:unit])
    y["AE"] = across(after(x["A"], y["AM"]))
    x["AM"] = trade(either(own("C1", trade), y["AM"]))
    y["BM"] = across(own("B", across))
    x["AE"] = trade(either(own("C2", trade), y["AE"]))
    y["C1M"] = across(own("C1", across))
    x["BM"] = trade(either(guest(0, trade), y["BM"]))
    y["C2M"] = across(own("C2", across))
    x["C1M"] = trade(either(guest(1, trade), y["C1M"]))
    y["C3M"] = across(own("C3", across))
    x["C2M"] = trade(either(guest(2, trade), y["C2M"]))
    y["BE"] = across(across.ready(x["B"]))
    x["C3M"] = trade(either(own("C3", trade), y["C3M"]))
    y["C1E"] = across(across.ready(x["AM"]))
    x["BE"] = trade(either(guest(3, trade), y["BE"]))
    y["C2E"] = across(across.ready(x["AE"]))
    x["C1E"] = trade(either(guest(4, trade), y["C1E"]))
    y["C3E"] = across(after(x["C3M"], y["C2E"]))
    x["C2E"] = trade(trade.ready(y["C2E"]), TO_END)
    x["C3E"] = trade(trade.ready(y["C3E"]), TO_END)

    proj_acts = dot(columns(after(acts, x["A"], y["AM"]), place, 0, unit), left)
    proj_acts += dot(columns(acts, near, 0, unit), x["A"])
    proj_acts += dot(columns(acts, far_middle, 0, unit), either(x["AM"], y["AM"]))
    proj_acts += dot(columns(acts, far_end, 0, unit), either(x["AE"], y["AE"]))
    other_acts = lax.ppermute(proj_acts, "mp", [(0, 1), (1, 0)])
    masked = after((proj_acts + other_acts) * live_rows(seq_len, row_count))
    guest_acts = lax.ppermute(masked, "dp", TO_MIDDLE)

    def near_term(name, got):
        if name != "B":
            got = either(jnp.zeros_like(got), got)
        return dot(columns(grads, near, *spans[name]), got)

    def middle_term(name):
        return dot(columns(grads, far_middle, *spans[name]), either(x[name + "M"], y[name + "M"]))

    def end_term(name):
        return dot(columns(grads, far_end, *spans[name]), either(x[name + "E"], y[name + "E"]))

    def guest_term(index, got):
        start = unit + index * half
        terms = []
        for block in (0, 1):
            rows = got[block * row_count : (block + 1) * row_count]
            begin = start + block * (half // 2)
            terms.append(dot(rows, right[begin : begin + half // 2]))
        return terms[0] + terms[1]

    proj_grads = dot(columns(after(grads, x["AM"], y["AE"]), place, 0, depth), right)
    proj_grads = after(proj_grads, x["AE"])
    proj_grads += near_term("B", x["B"])
    proj_grads = after(proj_grads)
    proj_grads += near_term("C1", x["AM"])
    proj_grads += near_term("C2", x["AE"])
    proj_grads = after(proj_grads)
    proj_grads += middle_term("B")
    guest_grads = guest_term(0, x["BM"])
    proj_grads += middle_term("C1")
    guest_grads += guest_term(1, x["C1M"])
    proj_grads, guest_grads = lax.optimization_barrier((proj_grads, guest_grads))
    proj_grads += middle_term("C2")
    guest_grads += guest_term(2, x["C2M"])
    proj_grads += middle_term("C3")
    proj_grads += near_term("C3", x["C3M"])
    proj_grads, guest_grads, masked = lax.optimization_barrier((proj_grads, guest_grads, masked))
    proj_grads += end_term("B")
    guest_grads += guest_term(3, x["BE"])
    proj_grads, guest_grads = lax.optimization_barrier((proj_grads, guest_grads))
    proj_grads += end_term("C1")
    guest_grads += guest_term(4, x["C1E"])
    guest_scores = lax.ppermute(column_scores(guest_acts, guest_grads, seq_count), "dp", TO_END)

    proj_grads = after(proj_grads)
    proj_grads = after(proj_grads + end_term("C2"), guest_scores)
    proj_grads += end_term("C3")
    scores = rank_scores(column_scores(masked, proj_grads, seq_count) + guest_scores)
    other_scores = lax.ppermute(scores, "mp", [(0, 1), (1, 0)])
    return (scores + other_scores) / math.sqrt(RANK * LEN)


def suits_line(mesh, acts, left, right):
    unit = left.shape[0]
    fits = right.shape[0] * 2 == unit * 7 and acts.shape[0] * 2 == unit and left.shape[1] * 4 == unit
    return mesh.shape["dp"] == 4 and mesh.shape["mp"] == 2 and fits


def solution(mesh):
    def on_device(acts, grads, query_left, query_right, seq_len):
        body = on_line if suits_line(mesh, acts[0], query_left[0], query_right[0]) else on_any
        return body(acts[0], grads[0], query_left[0], query_right[0], seq_len)[None]

    return jax.shard_map(
        on_device,
        mesh=mesh,
        in_specs=(
            P("layer", ("groups", "dp"), "mp"),
            P("layer", ("groups", "dp"), "mp"),
            P("layer", ("mp", "dp"), "groups"),
            P("layer", ("mp", "dp"), "groups"),
            P(("groups", "dp")),
        ),
        out_specs=P("layer", ("groups", "dp"), None),
        check_vma=False,
    )
```

```python
import math

import jax
import jax.numpy as jnp
from jax import lax
from jax.sharding import PartitionSpec as P

RANK = 8
LEN = 256

TRADE = [(0, 1), (1, 0), (2, 3), (3, 2)]
TO_END = [(1, 0), (2, 3)]
ACROSS = [(1, 2), (2, 1)]
TO_MIDDLE = [(0, 1), (3, 2)]


def live_rows(seq_len, row_count):
    seq_count = seq_len.shape[0]
    seq_span = row_count // seq_count
    positions = lax.broadcasted_iota(jnp.int32, (seq_count, seq_span, 1), 1)
    live = (positions < seq_len[:, None, None]).astype(jnp.float32)
    return live.reshape(row_count, 1)


def column_scores(masked_acts, proj_grads, seq_count):
    product = masked_acts * proj_grads
    return jnp.sum(product.reshape(seq_count, -1, product.shape[1]), axis=1)


def rank_scores(columns):
    seq_count = columns.shape[0]
    return jnp.sum(columns.reshape(seq_count, -1, RANK), axis=2)


def dot(a, b):
    return jnp.dot(a, b, preferred_element_type=jnp.float32)


def on_any(acts, grads, left, right, seq_len):
    seq_count = seq_len.shape[0]
    live = live_rows(seq_len, acts.shape[0])
    proj_acts = dot(acts, lax.all_gather(left, "dp", axis=0, tiled=True))
    proj_grads = dot(grads, lax.all_gather(right, "dp", axis=0, tiled=True))
    masked = lax.psum(proj_acts, "mp") * live
    scores = rank_scores(column_scores(masked, proj_grads, seq_count))
    return lax.psum(scores, "mp") / math.sqrt(RANK * LEN)


def after(value, *arrived):
    return lax.optimization_barrier((value, *arrived))[0]


class Sender:
    def __init__(self, pairs):
        self.pairs = pairs
        self.came = []

    def ready(self, value, *arrived):
        return after(value, *self.came[-2:-1], *arrived)

    def __call__(self, x, pairs=None):
        self.came.append(lax.ppermute(x, "dp", pairs or self.pairs))
        return self.came[-1]


def on_line(acts, grads, left, right, seq_len):
    seq_count = seq_len.shape[0]
    row_count = acts.shape[0]
    place = lax.axis_index("dp")
    is_end = (place == 0) | (place == 3)
    near = place ^ 1
    far_middle = jnp.where(place < 2, 2, 1)
    far_end = jnp.where(place < 2, 3, 0)

    unit = left.shape[0]
    depth = right.shape[0]
    half = unit // 2
    spans = {"B": (0, unit), "C": (unit, 2 * unit), "D": (2 * unit, depth)}
    trade = Sender(TRADE)
    across = Sender(ACROSS)

    def columns(array, source, start, stop):
        span = array.shape[1] // 4
        return lax.dynamic_slice_in_dim(array, source * span + start, stop - start, axis=1)

    def own(name, sender):
        start, stop = spans[name]
        return sender.ready(right)[start:stop]

    def guest_blocks(index, source):
        start = unit + index * half
        middle = start + half // 2
        return [columns(source, near, start, middle), columns(source, near, middle, start + half)]

    def guest(index, sender):
        return jnp.concatenate(guest_blocks(index, sender.ready(grads)), axis=0)

    def either(at_end, at_middle):
        return jnp.where(is_end, at_end, at_middle)

    x, y = {}, {}
    x["A"] = trade(left)
    y["AM"] = across(left)
    x["B"] = trade(right[:unit])
    y["AE"] = across(after(x["A"], y["AM"]))
    x["AM"] = trade(either(own("C", trade), y["AM"]))
    y["BM"] = across(own("B", across))
    x["AE"] = trade(either(trade.ready(right)[2 * unit : 3 * unit], y["AE"]))
    y["CM"] = across(own("C", across))
    x["BM"] = trade(either(guest(0, trade), y["BM"]))
    y["DM"] = across(own("D", across))
    x["CM"] = trade(either(guest(1, trade), y["CM"]))
    y["BE"] = across(across.ready(x["B"]))
    mixed = guest_blocks(2, trade.ready(grads)) + [right[3 * unit :]]
    x["DM"] = trade(either(jnp.concatenate(mixed, axis=0), y["DM"]))
    y["CE"] = across(across.ready(x["AM"]))
    x["BE"] = trade(either(guest(3, trade), y["BE"]))
    last = jnp.concatenate([across.ready(x["AE"]), x["DM"][unit:]], axis=0)
    y["DE"] = across(last)
    x["CE"] = trade(either(guest(4, trade), y["CE"]))
    x["DE"] = trade(trade.ready(y["DE"]), TO_END)

    proj_acts = dot(columns(after(acts, x["AM"]), place, 0, unit), left)
    proj_acts += dot(columns(acts, near, 0, unit), x["A"])
    proj_acts += dot(columns(acts, far_middle, 0, unit), either(x["AM"], y["AM"]))
    proj_acts += dot(columns(acts, far_end, 0, unit), either(x["AE"], y["AE"]))
    other_acts = lax.ppermute(proj_acts, "mp", [(0, 1), (1, 0)])
    masked = after((proj_acts + other_acts) * live_rows(seq_len, row_count))
    guest_acts = lax.ppermute(masked, "dp", TO_MIDDLE)

    def near_term(got, start, stop):
        got = either(jnp.zeros_like(got), got)
        return dot(columns(grads, near, start, stop), got)

    def middle_term(name):
        return dot(columns(grads, far_middle, *spans[name]), either(x[name + "M"], y[name + "M"]))

    def end_term(name):
        return dot(columns(grads, far_end, *spans[name]), either(x[name + "E"], y[name + "E"]))

    def guest_term(index, got):
        start = unit + index * half
        terms = []
        for block in (0, 1):
            rows = got[block * row_count : (block + 1) * row_count]
            begin = start + block * (half // 2)
            terms.append(dot(rows, right[begin : begin + half // 2]))
        return terms[0] + terms[1]

    proj_grads = dot(columns(after(grads, x["AE"]), place, 0, depth), right)
    proj_grads = after(proj_grads, x["AE"])
    proj_grads += dot(columns(grads, near, *spans["B"]), x["B"])
    proj_grads = after(proj_grads)
    proj_grads += near_term(x["AM"], unit, 2 * unit)
    proj_grads += near_term(x["AE"], 2 * unit, 3 * unit)
    proj_grads = after(proj_grads)
    proj_grads += middle_term("B")
    guest_grads = guest_term(0, x["BM"])
    proj_grads += middle_term("C")
    guest_grads += guest_term(1, x["CM"])
    proj_grads, guest_grads = lax.optimization_barrier((proj_grads, guest_grads))
    proj_grads += middle_term("D")
    guest_grads += guest_term(2, x["DM"])
    proj_grads += near_term(x["DM"][unit:], 3 * unit, depth)
    proj_grads, guest_grads, masked = lax.optimization_barrier((proj_grads, guest_grads, masked))
    proj_grads += end_term("B")
    guest_grads += guest_term(3, x["BE"])
    proj_grads, guest_grads = lax.optimization_barrier((proj_grads, guest_grads))
    proj_grads += end_term("C")
    guest_grads += guest_term(4, x["CE"])
    guest_scores = lax.ppermute(column_scores(guest_acts, guest_grads, seq_count), "dp", TO_END)

    proj_grads = after(proj_grads, guest_scores)
    proj_grads += end_term("D")
    scores = rank_scores(column_scores(masked, proj_grads, seq_count) + guest_scores)
    other_scores = lax.ppermute(scores, "mp", [(0, 1), (1, 0)])
    return (scores + other_scores) / math.sqrt(RANK * LEN)


def suits_line(mesh, acts, left, right):
    unit = left.shape[0]
    fits = right.shape[0] * 2 == unit * 7 and acts.shape[0] * 2 == unit and left.shape[1] * 4 == unit
    return mesh.shape["dp"] == 4 and mesh.shape["mp"] == 2 and fits


def solution(mesh):
    def on_device(acts, grads, query_left, query_right, seq_len):
        body = on_line if suits_line(mesh, acts[0], query_left[0], query_right[0]) else on_any
        return body(acts[0], grads[0], query_left[0], query_right[0], seq_len)[None]

    return jax.shard_map(
        on_device,
        mesh=mesh,
        in_specs=(
            P("layer", ("groups", "dp"), "mp"),
            P("layer", ("groups", "dp"), "mp"),
            P("layer", ("mp", "dp"), "groups"),
            P("layer", ("mp", "dp"), "groups"),
            P(("groups", "dp")),
        ),
        out_specs=P("layer", ("groups", "dp"), None),
        check_vma=False,
    )
```

```python
import math

import jax
import jax.numpy as jnp
from jax import lax
from jax.sharding import PartitionSpec as P

RANK = 8
LEN = 256

TRADE = [(0, 1), (1, 0), (2, 3), (3, 2)]
TO_END = [(1, 0), (2, 3)]
ACROSS = [(1, 2), (2, 1)]
TO_MIDDLE = [(0, 1), (3, 2)]


def live_rows(seq_len, row_count):
    seq_count = seq_len.shape[0]
    seq_span = row_count // seq_count
    positions = lax.broadcasted_iota(jnp.int32, (seq_count, seq_span, 1), 1)
    live = (positions < seq_len[:, None, None]).astype(jnp.float32)
    return live.reshape(row_count, 1)


def column_scores(masked_acts, proj_grads, seq_count):
    product = masked_acts * proj_grads
    return jnp.sum(product.reshape(seq_count, -1, product.shape[1]), axis=1)


def rank_scores(columns):
    seq_count = columns.shape[0]
    return jnp.sum(columns.reshape(seq_count, -1, RANK), axis=2)


def dot(a, b):
    return jnp.dot(a, b, preferred_element_type=jnp.float32)


def on_any(acts, grads, left, right, seq_len):
    seq_count = seq_len.shape[0]
    live = live_rows(seq_len, acts.shape[0])
    proj_acts = dot(acts, lax.all_gather(left, "dp", axis=0, tiled=True))
    proj_grads = dot(grads, lax.all_gather(right, "dp", axis=0, tiled=True))
    masked = lax.psum(proj_acts, "mp") * live
    scores = rank_scores(column_scores(masked, proj_grads, seq_count))
    return lax.psum(scores, "mp") / math.sqrt(RANK * LEN)


def after(value, *arrived):
    return lax.optimization_barrier((value, *arrived))[0]


class Sender:
    def __init__(self, pairs):
        self.pairs = pairs
        self.came = []

    def ready(self, value, *arrived):
        return after(value, *self.came[-2:-1], *arrived)

    def __call__(self, x, pairs=None):
        self.came.append(lax.ppermute(x, "dp", pairs or self.pairs))
        return self.came[-1]

    def gather(self, x):
        both = lax.all_gather(x, "dp", axis_index_groups=[[0, 1], [2, 3]])
        other = (lax.axis_index("dp") & 1) ^ 1
        self.came.append(lax.dynamic_index_in_dim(both, other, 0, keepdims=False))
        return self.came[-1]


def on_line(acts, grads, left, right, seq_len):
    seq_count = seq_len.shape[0]
    row_count = acts.shape[0]
    place = lax.axis_index("dp")
    is_end = (place == 0) | (place == 3)
    near = place ^ 1
    far_middle = jnp.where(place < 2, 2, 1)
    far_end = jnp.where(place < 2, 3, 0)

    unit = left.shape[0]
    depth = right.shape[0]
    half = unit // 2
    spans = {"B": (0, unit), "C1": (unit, 2 * unit), "C2": (2 * unit, 3 * unit), "C3": (3 * unit, depth)}
    trade = Sender(TRADE)
    across = Sender(ACROSS)

    def columns(array, source, start, stop):
        span = array.shape[1] // 4
        return lax.dynamic_slice_in_dim(array, source * span + start, stop - start, axis=1)

    def own(name, sender):
        start, stop = spans[name]
        return sender.ready(right)[start:stop]

    def guest(index, sender):
        source = sender.ready(grads)
        start = unit + index * half
        middle = start + half // 2
        blocks = [columns(source, near, start, middle), columns(source, near, middle, start + half)]
        return jnp.concatenate(blocks, axis=0)

    def either(at_end, at_middle):
        return jnp.where(is_end, at_end, at_middle)

    x, y = {}, {}
    x["A"] = trade(left)
    y["AM"] = across(left)
    x["B"] = trade(right[:unit])
    y["AE"] = across(after(x["A"], y["AM"]))
    x["AM"] = trade(either(own("C1", trade), y["AM"]))
    y["BM"] = across(own("B", across))
    x["AE"] = trade(either(own("C2", trade), y["AE"]))
    y["C1M"] = across(own("C1", across))
    x["BM"] = trade.gather(either(guest(0, trade), y["BM"]))
    y["C2M"] = across(own("C2", across))
    x["C1M"] = trade(either(guest(1, trade), y["C1M"]))
    y["C3M"] = across(own("C3", across))
    x["C2M"] = trade.gather(either(guest(2, trade), y["C2M"]))
    y["BE"] = across(across.ready(x["B"]))
    x["C3M"] = trade(either(own("C3", trade), y["C3M"]))
    y["C1E"] = across(across.ready(x["AM"]))
    x["BE"] = trade.gather(either(guest(3, trade), y["BE"]))
    y["C2E"] = across(across.ready(x["AE"]))
    x["C1E"] = trade(either(guest(4, trade), y["C1E"]))
    y["C3E"] = across(after(x["C3M"], y["C2E"]))
    x["C2E"] = trade(trade.ready(y["C2E"]), TO_END)
    x["C3E"] = trade(trade.ready(y["C3E"]), TO_END)

    proj_acts = dot(columns(after(acts, x["A"], y["AM"]), place, 0, unit), left)
    proj_acts += dot(columns(acts, near, 0, unit), x["A"])
    proj_acts += dot(columns(acts, far_middle, 0, unit), either(x["AM"], y["AM"]))
    proj_acts += dot(columns(acts, far_end, 0, unit), either(x["AE"], y["AE"]))
    other_acts = lax.ppermute(proj_acts, "mp", [(0, 1), (1, 0)])
    masked = after((proj_acts + other_acts) * live_rows(seq_len, row_count))
    guest_acts = lax.ppermute(masked, "dp", TO_MIDDLE)

    def near_term(name, got):
        if name != "B":
            got = either(jnp.zeros_like(got), got)
        return dot(columns(grads, near, *spans[name]), got)

    def middle_term(name):
        return dot(columns(grads, far_middle, *spans[name]), either(x[name + "M"], y[name + "M"]))

    def end_term(name):
        return dot(columns(grads, far_end, *spans[name]), either(x[name + "E"], y[name + "E"]))

    def guest_term(index, got):
        start = unit + index * half
        terms = []
        for block in (0, 1):
            rows = got[block * row_count : (block + 1) * row_count]
            begin = start + block * (half // 2)
            terms.append(dot(rows, right[begin : begin + half // 2]))
        return terms[0] + terms[1]

    proj_grads = dot(columns(after(grads, x["AM"], y["AE"]), place, 0, depth), right)
    proj_grads = after(proj_grads, x["AE"])
    proj_grads += near_term("B", x["B"])
    proj_grads = after(proj_grads)
    proj_grads += near_term("C1", x["AM"])
    proj_grads += near_term("C2", x["AE"])
    proj_grads = after(proj_grads)
    proj_grads += middle_term("B")
    guest_grads = guest_term(0, x["BM"])
    proj_grads += middle_term("C1")
    guest_grads += guest_term(1, x["C1M"])
    proj_grads, guest_grads = lax.optimization_barrier((proj_grads, guest_grads))
    proj_grads += middle_term("C2")
    guest_grads += guest_term(2, x["C2M"])
    proj_grads += middle_term("C3")
    proj_grads += near_term("C3", x["C3M"])
    proj_grads, guest_grads, masked = lax.optimization_barrier((proj_grads, guest_grads, masked))
    proj_grads += end_term("B")
    guest_grads += guest_term(3, x["BE"])
    proj_grads, guest_grads = lax.optimization_barrier((proj_grads, guest_grads))
    proj_grads += end_term("C1")
    guest_grads += guest_term(4, x["C1E"])
    guest_scores = lax.ppermute(column_scores(guest_acts, guest_grads, seq_count), "dp", TO_END)

    proj_grads = after(proj_grads)
    proj_grads = after(proj_grads + end_term("C2"), guest_scores)
    proj_grads += end_term("C3")
    scores = rank_scores(column_scores(masked, proj_grads, seq_count) + guest_scores)
    other_scores = lax.ppermute(scores, "mp", [(0, 1), (1, 0)])
    return (scores + other_scores) / math.sqrt(RANK * LEN)


def suits_line(mesh, acts, left, right):
    unit = left.shape[0]
    fits = right.shape[0] * 2 == unit * 7 and acts.shape[0] * 2 == unit and left.shape[1] * 4 == unit
    return mesh.shape["dp"] == 4 and mesh.shape["mp"] == 2 and fits


def solution(mesh):
    def on_device(acts, grads, query_left, query_right, seq_len):
        body = on_line if suits_line(mesh, acts[0], query_left[0], query_right[0]) else on_any
        return body(acts[0], grads[0], query_left[0], query_right[0], seq_len)[None]

    return jax.shard_map(
        on_device,
        mesh=mesh,
        in_specs=(
            P("layer", ("groups", "dp"), "mp"),
            P("layer", ("groups", "dp"), "mp"),
            P("layer", ("mp", "dp"), "groups"),
            P("layer", ("mp", "dp"), "groups"),
            P(("groups", "dp")),
        ),
        out_specs=P("layer", ("groups", "dp"), None),
        check_vma=False,
    )
```

```python
import math

import jax
import jax.numpy as jnp
from jax import lax
from jax.sharding import PartitionSpec as P

RANK = 8
LEN = 256

TRADE = [(0, 1), (1, 0), (2, 3), (3, 2)]
TO_END = [(1, 0), (2, 3)]
ACROSS = [(1, 2), (2, 1)]
TO_MIDDLE = [(0, 1), (3, 2)]


def live_rows(seq_len, row_count):
    seq_count = seq_len.shape[0]
    seq_span = row_count // seq_count
    positions = lax.broadcasted_iota(jnp.int32, (seq_count, seq_span, 1), 1)
    live = (positions < seq_len[:, None, None]).astype(jnp.float32)
    return live.reshape(row_count, 1)


def column_scores(masked_acts, proj_grads, seq_count):
    product = masked_acts * proj_grads
    return jnp.sum(product.reshape(seq_count, -1, product.shape[1]), axis=1)


def rank_scores(columns):
    seq_count = columns.shape[0]
    return jnp.sum(columns.reshape(seq_count, -1, RANK), axis=2)


def dot(a, b):
    return jnp.dot(a, b, preferred_element_type=jnp.float32)


def on_any(acts, grads, left, right, seq_len):
    seq_count = seq_len.shape[0]
    live = live_rows(seq_len, acts.shape[0])
    proj_acts = dot(acts, lax.all_gather(left, "dp", axis=0, tiled=True))
    proj_grads = dot(grads, lax.all_gather(right, "dp", axis=0, tiled=True))
    masked = lax.psum(proj_acts, "mp") * live
    scores = rank_scores(column_scores(masked, proj_grads, seq_count))
    return lax.psum(scores, "mp") / math.sqrt(RANK * LEN)


def after(value, *arrived):
    return lax.optimization_barrier((value, *arrived))[0]


class Sender:
    def __init__(self, pairs):
        self.pairs = pairs
        self.came = []

    def ready(self, value, *arrived):
        return after(value, *self.came[-3:-1], *arrived)

    def __call__(self, x, pairs=None):
        self.came.append(lax.ppermute(x, "dp", pairs or self.pairs))
        return self.came[-1]


def on_line(acts, grads, left, right, seq_len):
    seq_count = seq_len.shape[0]
    row_count = acts.shape[0]
    place = lax.axis_index("dp")
    is_end = (place == 0) | (place == 3)
    near = place ^ 1
    far_middle = jnp.where(place < 2, 2, 1)
    far_end = jnp.where(place < 2, 3, 0)

    unit = left.shape[0]
    depth = right.shape[0]
    width = left.shape[1]
    kept = 3 * unit // 4
    spans = {"B": (0, kept), "C1": (kept, kept + unit), "C2": (kept + unit, kept + 2 * unit), "C3": (kept + 2 * unit, depth)}
    shares = [kept // 2, unit // 2, unit // 2, kept // 2, unit // 2, unit // 2]
    guests = [(kept + sum(shares[:i]), kept + sum(shares[: i + 1])) for i in range(len(shares))]
    trade = Sender(TRADE)
    across = Sender(ACROSS)

    def columns(array, source, start, stop):
        span = array.shape[1] // 4
        return lax.dynamic_slice_in_dim(array, source * span + start, stop - start, axis=1)

    def own(name, sender):
        start, stop = spans[name]
        return sender.ready(right)[start:stop]

    def guest(index, sender):
        source = sender.ready(grads)
        start, stop = guests[index]
        blocks = []
        while start < stop:
            block = columns(source, near, start, min(start + width, stop))
            start += width
            parts = width // block.shape[1]
            blocks.append(jnp.concatenate(jnp.split(block, parts, axis=0), axis=1))
        return jnp.concatenate(blocks, axis=0)

    def either(at_end, at_middle):
        return jnp.where(is_end, at_end, at_middle)

    x, y = {}, {}
    x["A"] = trade(left)
    y["AM"] = across(left)
    x["B"] = trade(right[:kept])
    y["AE"] = across(after(x["A"], y["AM"]))
    x["AM"] = trade(either(own("C1", trade), y["AM"]))
    y["BM"] = across(own("B", across))
    x["AE"] = trade(either(own("C2", trade), y["AE"]))
    y["C1M"] = across(own("C1", across))
    x["BM"] = trade(either(guest(0, trade), y["BM"]))
    y["C2M"] = across(own("C2", across))
    x["C1M"] = trade(either(guest(1, trade), y["C1M"]))
    y["C3M"] = across(own("C3", across))
    x["C2M"] = trade(either(guest(2, trade), y["C2M"]))
    y["BE"] = across(across.ready(x["B"]))
    x["C3M"] = trade(either(own("C3", trade), y["C3M"]))
    y["C1E"] = across(across.ready(x["AM"]))
    x["BE"] = trade(either(guest(3, trade), y["BE"]))
    y["C2E"] = across(across.ready(x["AE"]))
    x["C1E"] = trade(either(guest(4, trade), y["C1E"]))
    y["C3E"] = across(after(x["C3M"], y["C2E"]))
    x["C2E"] = trade(either(guest(5, trade), y["C2E"]))
    x["C3E"] = trade(y["C3E"], TO_END)

    x["BM"] = after(x["BM"], x["AE"])
    proj_acts = dot(columns(after(acts, x["A"], y["AM"]), place, 0, unit), left)
    proj_acts += dot(columns(acts, near, 0, unit), x["A"])
    proj_acts += dot(columns(acts, far_middle, 0, unit), either(x["AM"], y["AM"]))
    proj_acts += dot(columns(acts, far_end, 0, unit), either(x["AE"], y["AE"]))
    other_acts = lax.ppermute(proj_acts, "mp", [(0, 1), (1, 0)])
    masked = after((proj_acts + other_acts) * live_rows(seq_len, row_count))
    by_seq = masked.reshape(seq_count, -1, width)
    scale = jnp.maximum(jnp.max(jnp.abs(by_seq), axis=1, keepdims=True), 1e-30) / 32767
    coded = jnp.round(by_seq / scale).astype(jnp.int16).reshape(row_count, width)
    guest_acts = lax.ppermute(coded, "dp", TO_MIDDLE)

    def near_term(name, got):
        if name != "B":
            got = either(jnp.zeros_like(got), got)
        return dot(columns(grads, near, *spans[name]), got)

    def middle_term(name):
        return dot(columns(grads, far_middle, *spans[name]), either(x[name + "M"], y[name + "M"]))

    def end_term(name):
        return dot(columns(grads, far_end, *spans[name]), either(x[name + "E"], y[name + "E"]))

    def guest_term(index, got):
        start, stop = guests[index]
        total = None
        while start < stop:
            span = min(width, stop - start)
            rows = row_count * span // width
            block = jnp.concatenate(jnp.split(got[:rows], width // span, axis=1), axis=0)
            got = got[rows:]
            term = dot(block, right[start : start + span])
            total = term if total is None else total + term
            start += span
        return total

    proj_grads = dot(columns(after(grads, x["AE"]), place, 0, depth), right)
    proj_grads = after(proj_grads, x["AE"])
    proj_grads += near_term("B", after(x["B"], x["AM"], y["AE"]))
    proj_grads = after(proj_grads)
    proj_grads += near_term("C1", after(x["AM"], x["AE"]))
    proj_grads += near_term("C2", x["AE"])
    proj_grads = after(proj_grads)
    proj_grads += middle_term("B")
    guest_grads = guest_term(0, x["BM"])
    proj_grads += middle_term("C1")
    guest_grads += guest_term(1, x["C1M"])
    proj_grads, guest_grads = lax.optimization_barrier((proj_grads, guest_grads))
    proj_grads += middle_term("C2")
    guest_grads += guest_term(2, x["C2M"])
    proj_grads += middle_term("C3")
    proj_grads += near_term("C3", x["C3M"])
    proj_grads, guest_grads, masked = lax.optimization_barrier((proj_grads, guest_grads, masked))
    proj_grads += end_term("B")
    guest_grads += guest_term(3, x["BE"])
    proj_grads, guest_grads = lax.optimization_barrier((proj_grads, guest_grads))
    proj_grads += end_term("C1")
    guest_grads += guest_term(4, x["C1E"])
    proj_grads, guest_grads = lax.optimization_barrier((proj_grads, guest_grads))
    proj_grads += end_term("C2")
    guest_grads += guest_term(5, x["C2E"])
    guest_sums = column_scores(guest_acts.astype(jnp.float32), guest_grads, seq_count)
    guest_scores = lax.ppermute(guest_sums, "dp", TO_END) * scale[:, 0]

    proj_grads = after(proj_grads)
    proj_grads += end_term("C3")
    scores = rank_scores(column_scores(masked, proj_grads, seq_count) + guest_scores)
    other_scores = lax.ppermute(scores, "mp", [(0, 1), (1, 0)])
    return (scores + other_scores) / math.sqrt(RANK * LEN)


def suits_line(mesh, acts, left, right):
    unit, width = left.shape
    fits = right.shape[0] * 2 == unit * 7 and acts.shape[0] == 2 * width and unit == 4 * width
    return mesh.shape["dp"] == 4 and mesh.shape["mp"] == 2 and fits


def solution(mesh):
    def on_device(acts, grads, query_left, query_right, seq_len):
        body = on_line if suits_line(mesh, acts[0], query_left[0], query_right[0]) else on_any
        return body(acts[0], grads[0], query_left[0], query_right[0], seq_len)[None]

    return jax.shard_map(
        on_device,
        mesh=mesh,
        in_specs=(
            P("layer", ("groups", "dp"), "mp"),
            P("layer", ("groups", "dp"), "mp"),
            P("layer", ("mp", "dp"), "groups"),
            P("layer", ("mp", "dp"), "groups"),
            P(("groups", "dp")),
        ),
        out_specs=P("layer", ("groups", "dp"), None),
        check_vma=False,
    )
```

```python
import math

import jax
import jax.numpy as jnp
from jax import lax
from jax.sharding import PartitionSpec as P

RANK = 8
LEN = 256

TRADE = [(0, 1), (1, 0), (2, 3), (3, 2)]
TO_END = [(1, 0), (2, 3)]
ACROSS = [(1, 2), (2, 1)]
TO_MIDDLE = [(0, 1), (3, 2)]


def live_rows(seq_len, row_count):
    seq_count = seq_len.shape[0]
    seq_span = row_count // seq_count
    positions = lax.broadcasted_iota(jnp.int32, (seq_count, seq_span, 1), 1)
    live = (positions < seq_len[:, None, None]).astype(jnp.float32)
    return live.reshape(row_count, 1)


def column_scores(masked_acts, proj_grads, seq_count):
    product = masked_acts * proj_grads
    return jnp.sum(product.reshape(seq_count, -1, product.shape[1]), axis=1)


def rank_scores(columns):
    seq_count = columns.shape[0]
    return jnp.sum(columns.reshape(seq_count, -1, RANK), axis=2)


def dot(a, b):
    return jnp.dot(a, b, preferred_element_type=jnp.float32)


def on_any(acts, grads, left, right, seq_len):
    seq_count = seq_len.shape[0]
    live = live_rows(seq_len, acts.shape[0])
    proj_acts = dot(acts, lax.all_gather(left, "dp", axis=0, tiled=True))
    proj_grads = dot(grads, lax.all_gather(right, "dp", axis=0, tiled=True))
    masked = lax.psum(proj_acts, "mp") * live
    scores = rank_scores(column_scores(masked, proj_grads, seq_count))
    return lax.psum(scores, "mp") / math.sqrt(RANK * LEN)


def after(value, *arrived):
    return lax.optimization_barrier((value, *arrived))[0]


class Sender:
    def __init__(self, pairs):
        self.pairs = pairs
        self.came = []

    def ready(self, value, *arrived):
        return after(value, *self.came[-3:-1], *arrived)

    def __call__(self, x, pairs=None):
        self.came.append(lax.ppermute(x, "dp", pairs or self.pairs))
        return self.came[-1]


def on_line(acts, grads, left, right, seq_len):
    seq_count = seq_len.shape[0]
    row_count = acts.shape[0]
    place = lax.axis_index("dp")
    is_end = (place == 0) | (place == 3)
    near = place ^ 1
    far_middle = jnp.where(place < 2, 2, 1)
    far_end = jnp.where(place < 2, 3, 0)

    unit = left.shape[0]
    depth = right.shape[0]
    width = left.shape[1]
    kept = 3 * unit // 4
    spans = {"B": (0, kept), "C1": (kept, kept + unit), "C2": (kept + unit, kept + 2 * unit), "C3": (kept + 2 * unit, depth)}
    shares = [kept // 2, unit // 2, unit // 2, kept // 2, unit // 2, unit // 2]
    guests = [(kept + sum(shares[:i]), kept + sum(shares[: i + 1])) for i in range(len(shares))]
    trade = Sender(TRADE)
    across = Sender(ACROSS)

    def columns(array, source, start, stop):
        span = array.shape[1] // 4
        return lax.dynamic_slice_in_dim(array, source * span + start, stop - start, axis=1)

    def own(name, sender):
        start, stop = spans[name]
        return sender.ready(right)[start:stop]

    def guest(index, sender):
        source = sender.ready(grads)
        start, stop = guests[index]
        blocks = []
        while start < stop:
            block = columns(source, near, start, min(start + width, stop))
            start += width
            parts = width // block.shape[1]
            blocks.append(jnp.concatenate(jnp.split(block, parts, axis=0), axis=1))
        return jnp.concatenate(blocks, axis=0)

    def either(at_end, at_middle):
        return jnp.where(is_end, at_end, at_middle)

    x, y = {}, {}
    x["A"] = trade(left)
    y["AM"] = across(left)
    x["B"] = trade(right[:kept])
    y["AE"] = across(x["A"])
    x["AM"] = trade(either(own("C1", trade), y["AM"]))
    y["BM"] = across(own("B", across))
    x["AE"] = trade(either(own("C2", trade), y["AE"]))
    y["C1M"] = across(own("C1", across))
    x["BM"] = trade(either(guest(0, trade), y["BM"]))
    y["C2M"] = across(own("C2", across))
    x["C1M"] = trade(either(guest(1, trade), y["C1M"]))
    y["C3M"] = across(own("C3", across))
    x["C2M"] = trade(either(guest(2, trade), y["C2M"]))
    y["BE"] = across(across.ready(x["B"]))
    x["C3M"] = trade(either(own("C3", trade), y["C3M"]))
    y["C1E"] = across(across.ready(x["AM"]))
    x["BE"] = trade(either(guest(3, trade), y["BE"]))
    y["C2E"] = across(across.ready(x["AE"]))
    x["C1E"] = trade(either(guest(4, trade), y["C1E"]))
    y["C3E"] = across(after(x["C3M"], y["C2E"]))
    x["C2E"] = trade(either(guest(5, trade), y["C2E"]))
    x["C3E"] = trade(y["C3E"], TO_END)

    x["BM"] = after(x["BM"], x["AE"])
    x["AM"] = after(x["AM"], x["AE"])
    proj_acts = dot(columns(after(acts, x["A"], y["AM"]), place, 0, unit), left)
    proj_acts += dot(columns(acts, near, 0, unit), x["A"])
    proj_acts += dot(columns(acts, far_middle, 0, unit), either(x["AM"], y["AM"]))
    proj_acts += dot(columns(acts, far_end, 0, unit), either(x["AE"], y["AE"]))
    other_acts = lax.ppermute(proj_acts, "mp", [(0, 1), (1, 0)])
    masked = after((proj_acts + other_acts) * live_rows(seq_len, row_count))
    by_seq = masked.reshape(seq_count, -1, width)
    scale = jnp.maximum(jnp.max(jnp.abs(by_seq), axis=1, keepdims=True), 1e-30) / 32767
    coded = jnp.round(by_seq / scale).astype(jnp.int16).reshape(row_count, width)
    guest_acts = lax.ppermute(coded, "dp", TO_MIDDLE)

    def near_term(name, got):
        if name != "B":
            got = either(jnp.zeros_like(got), got)
        return dot(columns(grads, near, *spans[name]), got)

    def middle_term(name):
        return dot(columns(grads, far_middle, *spans[name]), either(x[name + "M"], y[name + "M"]))

    def end_term(name):
        return dot(columns(grads, far_end, *spans[name]), either(x[name + "E"], y[name + "E"]))

    def guest_term(index, got):
        start, stop = guests[index]
        total = None
        while start < stop:
            span = min(width, stop - start)
            rows = row_count * span // width
            block = jnp.concatenate(jnp.split(got[:rows], width // span, axis=1), axis=0)
            got = got[rows:]
            term = dot(block, right[start : start + span])
            total = term if total is None else total + term
            start += span
        return total

    proj_grads = dot(columns(after(grads, x["AE"]), place, 0, depth), right)
    proj_grads = after(proj_grads, x["AE"])
    proj_grads += near_term("B", after(x["B"], x["AM"], y["AE"]))
    proj_grads = after(proj_grads)
    proj_grads += near_term("C1", after(x["AM"], x["AE"]))
    proj_grads += near_term("C2", x["AE"])
    proj_grads = after(proj_grads)
    proj_grads += middle_term("B")
    guest_grads = guest_term(0, x["BM"])
    proj_grads += middle_term("C1")
    guest_grads += guest_term(1, x["C1M"])
    proj_grads, guest_grads = lax.optimization_barrier((proj_grads, guest_grads))
    proj_grads += middle_term("C2")
    guest_grads += guest_term(2, x["C2M"])
    proj_grads += middle_term("C3")
    proj_grads += near_term("C3", x["C3M"])
    proj_grads, guest_grads, masked = lax.optimization_barrier((proj_grads, guest_grads, masked))
    proj_grads += end_term("B")
    guest_grads += guest_term(3, x["BE"])
    proj_grads, guest_grads = lax.optimization_barrier((proj_grads, guest_grads))
    proj_grads += end_term("C1")
    guest_grads += guest_term(4, x["C1E"])
    proj_grads, guest_grads = lax.optimization_barrier((proj_grads, guest_grads))
    proj_grads += end_term("C2")
    guest_grads += guest_term(5, x["C2E"])
    guest_sums = column_scores(guest_acts.astype(jnp.float32), guest_grads, seq_count)
    guest_scores = lax.ppermute(guest_sums, "dp", TO_END) * scale[:, 0]

    proj_grads = after(proj_grads)
    proj_grads += end_term("C3")
    scores = rank_scores(column_scores(masked, proj_grads, seq_count) + guest_scores)
    other_scores = lax.ppermute(scores, "mp", [(0, 1), (1, 0)])
    return (scores + other_scores) / math.sqrt(RANK * LEN)


def suits_line(mesh, acts, left, right):
    unit, width = left.shape
    fits = right.shape[0] * 2 == unit * 7 and acts.shape[0] == 2 * width and unit == 4 * width
    return mesh.shape["dp"] == 4 and mesh.shape["mp"] == 2 and fits


def solution(mesh):
    def on_device(acts, grads, query_left, query_right, seq_len):
        body = on_line if suits_line(mesh, acts[0], query_left[0], query_right[0]) else on_any
        return body(acts[0], grads[0], query_left[0], query_right[0], seq_len)[None]

    return jax.shard_map(
        on_device,
        mesh=mesh,
        in_specs=(
            P("layer", ("groups", "dp"), "mp"),
            P("layer", ("groups", "dp"), "mp"),
            P("layer", ("mp", "dp"), "groups"),
            P("layer", ("mp", "dp"), "groups"),
            P(("groups", "dp")),
        ),
        out_specs=P("layer", ("groups", "dp"), None),
        check_vma=False,
    )
```

```python
import math

import jax
import jax.numpy as jnp
from jax import lax
from jax.sharding import PartitionSpec as P

RANK = 8
LEN = 256

TRADE = [(0, 1), (1, 0), (2, 3), (3, 2)]
TO_END = [(1, 0), (2, 3)]
ACROSS = [(1, 2), (2, 1)]
TO_MIDDLE = [(0, 1), (3, 2)]


def live_rows(seq_len, row_count):
    seq_count = seq_len.shape[0]
    seq_span = row_count // seq_count
    positions = lax.broadcasted_iota(jnp.int32, (seq_count, seq_span, 1), 1)
    live = (positions < seq_len[:, None, None]).astype(jnp.float32)
    return live.reshape(row_count, 1)


def column_scores(masked_acts, proj_grads, seq_count):
    product = masked_acts * proj_grads
    return jnp.sum(product.reshape(seq_count, -1, product.shape[1]), axis=1)


def rank_scores(columns):
    seq_count = columns.shape[0]
    return jnp.sum(columns.reshape(seq_count, -1, RANK), axis=2)


def dot(a, b):
    return jnp.dot(a, b, preferred_element_type=jnp.float32)


def on_any(acts, grads, left, right, seq_len):
    seq_count = seq_len.shape[0]
    live = live_rows(seq_len, acts.shape[0])
    proj_acts = dot(acts, lax.all_gather(left, "dp", axis=0, tiled=True))
    proj_grads = dot(grads, lax.all_gather(right, "dp", axis=0, tiled=True))
    masked = lax.psum(proj_acts, "mp") * live
    scores = rank_scores(column_scores(masked, proj_grads, seq_count))
    return lax.psum(scores, "mp") / math.sqrt(RANK * LEN)


def after(value, *arrived):
    return lax.optimization_barrier((value, *arrived))[0]


class Sender:
    def __init__(self, pairs):
        self.pairs = pairs
        self.came = []

    def ready(self, value, *arrived):
        return after(value, *self.came[-3:-1], *arrived)

    def __call__(self, x, pairs=None):
        self.came.append(lax.ppermute(x, "dp", pairs or self.pairs))
        return self.came[-1]


def on_line(acts, grads, left, right, seq_len):
    seq_count = seq_len.shape[0]
    row_count = acts.shape[0]
    place = lax.axis_index("dp")
    is_end = (place == 0) | (place == 3)
    near = place ^ 1
    far_middle = jnp.where(place < 2, 2, 1)
    far_end = jnp.where(place < 2, 3, 0)

    unit = left.shape[0]
    depth = right.shape[0]
    width = left.shape[1]
    kept = 3 * unit // 4
    spans = {"B": (0, kept), "C1": (kept, kept + unit), "C2": (kept + unit, kept + 2 * unit), "C3": (kept + 2 * unit, depth)}
    shares = [kept // 2, unit // 2, unit // 2, kept // 2, unit // 2, unit // 2]
    guests = [(kept + sum(shares[:i]), kept + sum(shares[: i + 1])) for i in range(len(shares))]
    trade = Sender(TRADE)
    across = Sender(ACROSS)

    def columns(array, source, start, stop):
        span = array.shape[1] // 4
        return lax.dynamic_slice_in_dim(array, source * span + start, stop - start, axis=1)

    def own(name, sender):
        start, stop = spans[name]
        return sender.ready(right)[start:stop]

    def guest(index, sender):
        source = sender.ready(grads)
        start, stop = guests[index]
        blocks = []
        while start < stop:
            block = columns(source, near, start, min(start + width, stop))
            start += width
            parts = width // block.shape[1]
            blocks.append(jnp.concatenate(jnp.split(block, parts, axis=0), axis=1))
        return jnp.concatenate(blocks, axis=0)

    def either(at_end, at_middle):
        return jnp.where(is_end, at_end, at_middle)

    x, y = {}, {}
    x["A"] = trade(left)
    y["AM"] = across(left)
    x["B"] = trade(right[:kept])
    y["AE"] = across(x["A"])
    x["AM"] = trade(either(own("C1", trade), y["AM"]))
    y["BM"] = across(own("B", across))
    x["AE"] = trade(either(own("C2", trade), y["AE"]))
    y["C1M"] = across(own("C1", across))
    x["BM"] = trade(either(guest(0, trade), y["BM"]))
    y["C2M"] = across(own("C2", across))
    x["C1M"] = trade(either(guest(1, trade), y["C1M"]))
    y["C3M"] = across(own("C3", across))
    x["C2M"] = trade(either(guest(2, trade), y["C2M"]))
    y["BE"] = across(across.ready(x["B"]))
    x["C3M"] = trade(either(own("C3", trade), y["C3M"]))
    y["C1E"] = across(across.ready(x["AM"]))
    x["BE"] = trade(either(guest(3, trade), y["BE"]))
    y["C2E"] = across(across.ready(x["AE"]))
    x["C1E"] = trade(either(guest(4, trade), y["C1E"]))
    y["C3E"] = across(after(x["C3M"], y["C2E"]))
    x["C2E"] = trade(either(guest(5, trade), y["C2E"]))
    x["C3E"] = trade(after(y["C3E"], x["C1E"]), TO_END)

    x["BM"] = after(x["BM"], x["AE"])
    x["AM"] = after(x["AM"], x["AE"])
    proj_acts = dot(columns(after(acts, x["A"], y["AM"]), place, 0, unit), left)
    proj_acts += dot(columns(acts, near, 0, unit), x["A"])
    proj_acts += dot(columns(acts, far_middle, 0, unit), either(x["AM"], y["AM"]))
    proj_acts += dot(columns(acts, far_end, 0, unit), either(x["AE"], y["AE"]))
    other_acts = lax.ppermute(proj_acts, "mp", [(0, 1), (1, 0)])
    masked = after((proj_acts + other_acts) * live_rows(seq_len, row_count))
    by_seq = masked.reshape(seq_count, -1, width)
    scale = jnp.maximum(jnp.max(jnp.abs(by_seq), axis=1, keepdims=True), 1e-30) / 32767
    coded = jnp.round(by_seq / scale).astype(jnp.int16).reshape(row_count, width)
    guest_acts = lax.ppermute(coded, "dp", TO_MIDDLE)

    def near_term(name, got):
        if name != "B":
            got = either(jnp.zeros_like(got), got)
        return dot(columns(grads, near, *spans[name]), got)

    def middle_term(name):
        return dot(columns(grads, far_middle, *spans[name]), either(x[name + "M"], y[name + "M"]))

    def end_term(name):
        return dot(columns(grads, far_end, *spans[name]), either(x[name + "E"], y[name + "E"]))

    def guest_term(index, got):
        start, stop = guests[index]
        total = None
        while start < stop:
            span = min(width, stop - start)
            rows = row_count * span // width
            block = jnp.concatenate(jnp.split(got[:rows], width // span, axis=1), axis=0)
            got = got[rows:]
            term = dot(block, right[start : start + span])
            total = term if total is None else total + term
            start += span
        return total

    proj_grads = dot(columns(after(grads, x["AE"]), place, 0, depth), right)
    proj_grads = after(proj_grads, x["AE"])
    proj_grads += near_term("B", after(x["B"], x["AM"], y["AE"]))
    proj_grads = after(proj_grads)
    proj_grads += near_term("C1", after(x["AM"], x["AE"]))
    proj_grads += near_term("C2", x["AE"])
    proj_grads = after(proj_grads)
    proj_grads += middle_term("B")
    guest_grads = guest_term(0, x["BM"])
    proj_grads += middle_term("C1")
    guest_grads += guest_term(1, x["C1M"])
    proj_grads, guest_grads = lax.optimization_barrier((proj_grads, guest_grads))
    proj_grads += middle_term("C2")
    guest_grads += guest_term(2, x["C2M"])
    proj_grads += middle_term("C3")
    proj_grads += near_term("C3", x["C3M"])
    proj_grads, guest_grads, masked = lax.optimization_barrier((proj_grads, guest_grads, masked))
    proj_grads += end_term("B")
    guest_grads += guest_term(3, x["BE"])
    proj_grads, guest_grads = lax.optimization_barrier((proj_grads, guest_grads))
    proj_grads += end_term("C1")
    guest_grads += guest_term(4, x["C1E"])
    proj_grads, guest_grads = lax.optimization_barrier((proj_grads, guest_grads))
    guest_grads += guest_term(5, x["C2E"])
    guest_sums = column_scores(guest_acts.astype(jnp.float32), guest_grads, seq_count)
    guest_scores = lax.ppermute(guest_sums, "dp", TO_END) * scale[:, 0]

    proj_grads = after(proj_grads)
    proj_grads += end_term("C2") + end_term("C3")
    scores = rank_scores(column_scores(masked, proj_grads, seq_count) + guest_scores)
    other_scores = lax.ppermute(scores, "mp", [(0, 1), (1, 0)])
    return (scores + other_scores) / math.sqrt(RANK * LEN)


def suits_line(mesh, acts, left, right):
    unit, width = left.shape
    fits = right.shape[0] * 2 == unit * 7 and acts.shape[0] == 2 * width and unit == 4 * width
    return mesh.shape["dp"] == 4 and mesh.shape["mp"] == 2 and fits


def solution(mesh):
    def on_device(acts, grads, query_left, query_right, seq_len):
        body = on_line if suits_line(mesh, acts[0], query_left[0], query_right[0]) else on_any
        return body(acts[0], grads[0], query_left[0], query_right[0], seq_len)[None]

    return jax.shard_map(
        on_device,
        mesh=mesh,
        in_specs=(
            P("layer", ("groups", "dp"), "mp"),
            P("layer", ("groups", "dp"), "mp"),
            P("layer", ("mp", "dp"), "groups"),
            P("layer", ("mp", "dp"), "groups"),
            P(("groups", "dp")),
        ),
        out_specs=P("layer", ("groups", "dp"), None),
        check_vma=False,
    )
```

```python
import math

import jax
import jax.numpy as jnp
from jax import lax
from jax.sharding import PartitionSpec as P

RANK = 8
LEN = 256

TRADE = [(0, 1), (1, 0), (2, 3), (3, 2)]
TO_END = [(1, 0), (2, 3)]
ACROSS = [(1, 2), (2, 1)]
TO_MIDDLE = [(0, 1), (3, 2)]


def live_rows(seq_len, row_count):
    seq_count = seq_len.shape[0]
    seq_span = row_count // seq_count
    positions = lax.broadcasted_iota(jnp.int32, (seq_count, seq_span, 1), 1)
    live = (positions < seq_len[:, None, None]).astype(jnp.float32)
    return live.reshape(row_count, 1)


def column_scores(masked_acts, proj_grads, seq_count):
    product = masked_acts * proj_grads
    return jnp.sum(product.reshape(seq_count, -1, product.shape[1]), axis=1)


def rank_scores(columns):
    seq_count = columns.shape[0]
    return jnp.sum(columns.reshape(seq_count, -1, RANK), axis=2)


def dot(a, b):
    return jnp.dot(a, b, preferred_element_type=jnp.float32)


def on_any(acts, grads, left, right, seq_len):
    seq_count = seq_len.shape[0]
    live = live_rows(seq_len, acts.shape[0])
    proj_acts = dot(acts, lax.all_gather(left, "dp", axis=0, tiled=True))
    proj_grads = dot(grads, lax.all_gather(right, "dp", axis=0, tiled=True))
    masked = lax.psum(proj_acts, "mp") * live
    scores = rank_scores(column_scores(masked, proj_grads, seq_count))
    return lax.psum(scores, "mp") / math.sqrt(RANK * LEN)


def after(value, *arrived):
    return lax.optimization_barrier((value, *arrived))[0]


class Sender:
    def __init__(self, pairs):
        self.pairs = pairs
        self.came = []

    def ready(self, value, *arrived):
        return after(value, *self.came[-2:-1], *arrived)

    def __call__(self, x, pairs=None):
        self.came.append(lax.ppermute(x, "dp", pairs or self.pairs))
        return self.came[-1]


def on_line(acts, grads, left, right, seq_len):
    seq_count = seq_len.shape[0]
    row_count = acts.shape[0]
    place = lax.axis_index("dp")
    is_end = (place == 0) | (place == 3)
    near = place ^ 1
    far_middle = jnp.where(place < 2, 2, 1)
    far_end = jnp.where(place < 2, 3, 0)

    unit = left.shape[0]
    depth = right.shape[0]
    half = unit // 2
    spans = {"B": (0, unit), "C1": (unit, 2 * unit), "C2": (2 * unit, 3 * unit), "C3": (3 * unit, depth)}
    trade = Sender(TRADE)
    across = Sender(ACROSS)

    def columns(array, source, start, stop):
        span = array.shape[1] // 4
        return lax.dynamic_slice_in_dim(array, source * span + start, stop - start, axis=1)

    def own(name, sender):
        start, stop = spans[name]
        return sender.ready(right)[start:stop]

    def guest(index, sender):
        source = sender.ready(grads)
        start = unit + index * half
        middle = start + half // 2
        blocks = [columns(source, near, start, middle), columns(source, near, middle, start + half)]
        return jnp.concatenate(blocks, axis=0)

    def either(at_end, at_middle):
        return jnp.where(is_end, at_end, at_middle)

    x, y = {}, {}
    x["A"] = trade(left)
    y["AM"] = across(left)
    x["B"] = trade(right[:unit])
    y["AE"] = across(after(x["A"], y["AM"]))
    x["AM"] = trade(either(own("C1", trade), y["AM"]))
    y["BM"] = across(own("B", across))
    x["AE"] = trade(either(own("C2", trade), y["AE"]))
    y["C1M"] = across(own("C1", across))
    x["BM"] = trade(either(guest(0, trade), y["BM"]))
    y["C2M"] = across(own("C2", across))
    x["C1M"] = trade(either(guest(1, trade), y["C1M"]))
    y["C3M"] = across(own("C3", across))
    x["C2M"] = trade(either(guest(2, trade), y["C2M"]))
    y["BE"] = across(across.ready(x["B"]))
    x["C3M"] = trade(either(own("C3", trade), y["C3M"]))
    y["C1E"] = across(across.ready(x["AM"]))
    x["BE"] = trade(either(guest(3, trade), y["BE"]))
    y["C2E"] = across(across.ready(x["AE"]))
    x["C1E"] = trade(either(guest(4, trade), y["C1E"]))
    y["C3E"] = across(after(x["C3M"], y["C2E"]))
    x["C2E"] = trade(trade.ready(y["C2E"]), TO_END)
    x["C3E"] = trade(y["C3E"], TO_END)

    proj_acts = dot(columns(after(acts, x["A"], y["AM"]), place, 0, unit), left)
    proj_acts += dot(columns(acts, near, 0, unit), x["A"])
    proj_acts += dot(columns(acts, far_middle, 0, unit), either(x["AM"], y["AM"]))
    proj_acts += dot(columns(acts, far_end, 0, unit), either(x["AE"], y["AE"]))
    other_acts = lax.ppermute(proj_acts, "mp", [(0, 1), (1, 0)])
    masked = after((proj_acts + other_acts) * live_rows(seq_len, row_count))
    by_seq = masked.reshape(seq_count, -1, masked.shape[1])
    scale = jnp.maximum(jnp.max(jnp.abs(by_seq), axis=1, keepdims=True), 1e-30) / 32767
    coded = jnp.round(by_seq / scale).astype(jnp.int16).reshape(masked.shape)
    guest_acts = lax.ppermute(coded, "dp", TO_MIDDLE)

    def near_term(name, got):
        if name != "B":
            got = either(jnp.zeros_like(got), got)
        return dot(columns(grads, near, *spans[name]), got)

    def middle_term(name):
        return dot(columns(grads, far_middle, *spans[name]), either(x[name + "M"], y[name + "M"]))

    def end_term(name):
        return dot(columns(grads, far_end, *spans[name]), either(x[name + "E"], y[name + "E"]))

    def guest_term(index, got):
        start = unit + index * half
        terms = []
        for block in (0, 1):
            rows = got[block * row_count : (block + 1) * row_count]
            begin = start + block * (half // 2)
            terms.append(dot(rows, right[begin : begin + half // 2]))
        return terms[0] + terms[1]

    proj_grads = dot(columns(after(grads, x["AM"], y["AE"]), place, 0, depth), right)
    proj_grads = after(proj_grads, x["AE"])
    proj_grads += near_term("B", x["B"])
    proj_grads = after(proj_grads)
    proj_grads += near_term("C1", x["AM"])
    proj_grads += near_term("C2", x["AE"])
    proj_grads = after(proj_grads)
    proj_grads += middle_term("B")
    guest_grads = guest_term(0, x["BM"])
    proj_grads += middle_term("C1")
    guest_grads += guest_term(1, x["C1M"])
    proj_grads, guest_grads = lax.optimization_barrier((proj_grads, guest_grads))
    proj_grads += middle_term("C2")
    guest_grads += guest_term(2, x["C2M"])
    proj_grads += middle_term("C3")
    proj_grads += near_term("C3", x["C3M"])
    proj_grads, guest_grads, masked = lax.optimization_barrier((proj_grads, guest_grads, masked))
    proj_grads += end_term("B")
    guest_grads += guest_term(3, x["BE"])
    proj_grads, guest_grads = lax.optimization_barrier((proj_grads, guest_grads))
    proj_grads += end_term("C1")
    guest_grads += guest_term(4, x["C1E"])
    guest_scores = lax.ppermute(column_scores(guest_acts.astype(jnp.float32), guest_grads, seq_count), "dp", TO_END) * scale[:, 0]

    proj_grads = after(proj_grads)
    proj_grads = after(proj_grads + end_term("C2"), guest_scores)
    proj_grads += end_term("C3")
    scores = rank_scores(column_scores(masked, proj_grads, seq_count) + guest_scores)
    other_scores = lax.ppermute(scores, "mp", [(0, 1), (1, 0)])
    return (scores + other_scores) / math.sqrt(RANK * LEN)


def suits_line(mesh, acts, left, right):
    unit = left.shape[0]
    fits = right.shape[0] * 2 == unit * 7 and acts.shape[0] * 2 == unit and left.shape[1] * 4 == unit
    return mesh.shape["dp"] == 4 and mesh.shape["mp"] == 2 and fits


def solution(mesh):
    def on_device(acts, grads, query_left, query_right, seq_len):
        body = on_line if suits_line(mesh, acts[0], query_left[0], query_right[0]) else on_any
        return body(acts[0], grads[0], query_left[0], query_right[0], seq_len)[None]

    return jax.shard_map(
        on_device,
        mesh=mesh,
        in_specs=(
            P("layer", ("groups", "dp"), "mp"),
            P("layer", ("groups", "dp"), "mp"),
            P("layer", ("mp", "dp"), "groups"),
            P("layer", ("mp", "dp"), "groups"),
            P(("groups", "dp")),
        ),
        out_specs=P("layer", ("groups", "dp"), None),
        check_vma=False,
    )
```

```python
import math

import jax
import jax.numpy as jnp
from jax import lax
from jax.sharding import PartitionSpec as P

RANK = 8
LEN = 256

TRADE = [(0, 1), (1, 0), (2, 3), (3, 2)]
TO_END = [(1, 0), (2, 3)]
ACROSS = [(1, 2), (2, 1)]
TO_MIDDLE = [(0, 1), (3, 2)]


def live_rows(seq_len, row_count):
    seq_count = seq_len.shape[0]
    seq_span = row_count // seq_count
    positions = lax.broadcasted_iota(jnp.int32, (seq_count, seq_span, 1), 1)
    live = (positions < seq_len[:, None, None]).astype(jnp.float32)
    return live.reshape(row_count, 1)


def column_scores(masked_acts, proj_grads, seq_count):
    product = masked_acts * proj_grads
    return jnp.sum(product.reshape(seq_count, -1, product.shape[1]), axis=1)


def rank_scores(columns):
    seq_count = columns.shape[0]
    return jnp.sum(columns.reshape(seq_count, -1, RANK), axis=2)


def dot(a, b):
    return jnp.dot(a, b, preferred_element_type=jnp.float32)


def on_any(acts, grads, left, right, seq_len):
    seq_count = seq_len.shape[0]
    live = live_rows(seq_len, acts.shape[0])
    proj_acts = dot(acts, lax.all_gather(left, "dp", axis=0, tiled=True))
    proj_grads = dot(grads, lax.all_gather(right, "dp", axis=0, tiled=True))
    masked = lax.psum(proj_acts, "mp") * live
    scores = rank_scores(column_scores(masked, proj_grads, seq_count))
    return lax.psum(scores, "mp") / math.sqrt(RANK * LEN)


def after(value, *arrived):
    return lax.optimization_barrier((value, *arrived))[0]


class Sender:
    def __init__(self, pairs):
        self.pairs = pairs
        self.came = []

    def ready(self, value, *arrived):
        return after(value, *self.came[-2:-1], *arrived)

    def __call__(self, x, pairs=None):
        self.came.append(lax.ppermute(x, "dp", pairs or self.pairs))
        return self.came[-1]


def on_line(acts, grads, left, right, seq_len):
    seq_count = seq_len.shape[0]
    row_count = acts.shape[0]
    place = lax.axis_index("dp")
    is_end = (place == 0) | (place == 3)
    near = place ^ 1
    far_middle = jnp.where(place < 2, 2, 1)
    far_end = jnp.where(place < 2, 3, 0)

    unit = left.shape[0]
    depth = right.shape[0]
    half = unit // 2
    spans = {"B": (0, unit), "C1": (unit, 2 * unit), "C2": (2 * unit, 3 * unit), "C3": (3 * unit, depth)}
    trade = Sender(TRADE)
    across = Sender(ACROSS)

    def columns(array, source, start, stop):
        span = array.shape[1] // 4
        return lax.dynamic_slice_in_dim(array, source * span + start, stop - start, axis=1)

    def own(name, sender):
        start, stop = spans[name]
        return sender.ready(right)[start:stop]

    def guest(index, sender):
        source = sender.ready(grads)
        start = unit + index * half
        middle = start + half // 2
        blocks = [columns(source, near, start, middle), columns(source, near, middle, start + half)]
        return jnp.concatenate(blocks, axis=0)

    def either(at_end, at_middle):
        return jnp.where(is_end, at_end, at_middle)

    x, y = {}, {}
    x["A"] = trade(left)
    y["AM"] = across(left)
    x["B"] = trade(right[:unit])
    y["AE"] = across(after(x["A"], y["AM"]))
    x["AM"] = trade(either(own("C1", trade), y["AM"]))
    y["BM"] = across(own("B", across))
    x["AE"] = trade(either(own("C2", trade), y["AE"]))
    y["C1M"] = across(own("C1", across))
    x["BM"] = trade(either(guest(0, trade), y["BM"]))
    y["C2M"] = across(own("C2", across))
    x["C1M"] = trade(either(guest(1, trade), y["C1M"]))
    y["C3M"] = across(own("C3", across))
    x["C2M"] = trade(either(guest(2, trade), y["C2M"]))
    y["BE"] = across(across.ready(x["B"]))
    x["C3M"] = trade(either(own("C3", trade), y["C3M"]))
    y["C1E"] = across(across.ready(x["AM"]))
    x["BE"] = trade(either(guest(3, trade), y["BE"]))
    y["C2E"] = across(across.ready(x["AE"]))
    x["C1E"] = trade(either(guest(4, trade), y["C1E"]))
    y["C3E"] = across(after(x["C3M"], y["C2E"]))
    x["C2E"] = trade(trade.ready(y["C2E"]), TO_END)
    x["C3E"] = trade(y["C3E"], TO_END)

    x["C1E"] = after(x["C1E"], y["C3E"])

    proj_acts = dot(columns(after(acts, x["A"], y["AM"]), place, 0, unit), left)
    proj_acts += dot(columns(acts, near, 0, unit), x["A"])
    proj_acts += dot(columns(acts, far_middle, 0, unit), either(x["AM"], y["AM"]))
    proj_acts += dot(columns(acts, far_end, 0, unit), either(x["AE"], y["AE"]))
    other_acts = lax.ppermute(proj_acts, "mp", [(0, 1), (1, 0)])
    masked = after((proj_acts + other_acts) * live_rows(seq_len, row_count))
    by_seq = masked.reshape(seq_count, -1, masked.shape[1])
    scale = jnp.maximum(jnp.max(jnp.abs(by_seq), axis=1, keepdims=True), 1e-30) / 32767
    coded = jnp.round(by_seq / scale).astype(jnp.int16).reshape(masked.shape)
    guest_acts = lax.ppermute(coded, "dp", TO_MIDDLE)

    def near_term(name, got):
        if name != "B":
            got = either(jnp.zeros_like(got), got)
        return dot(columns(grads, near, *spans[name]), got)

    def middle_term(name):
        return dot(columns(grads, far_middle, *spans[name]), either(x[name + "M"], y[name + "M"]))

    def end_term(name):
        return dot(columns(grads, far_end, *spans[name]), either(x[name + "E"], y[name + "E"]))

    def guest_term(index, got):
        start = unit + index * half
        terms = []
        for block in (0, 1):
            rows = got[block * row_count : (block + 1) * row_count]
            begin = start + block * (half // 2)
            terms.append(dot(rows, right[begin : begin + half // 2]))
        return terms[0] + terms[1]

    proj_grads = dot(columns(after(grads, x["AM"], y["AE"]), place, 0, depth), right)
    proj_grads = after(proj_grads, x["AE"])
    proj_grads += near_term("B", x["B"])
    proj_grads = after(proj_grads)
    proj_grads += near_term("C1", x["AM"])
    proj_grads += near_term("C2", x["AE"])
    proj_grads = after(proj_grads)
    proj_grads += middle_term("B")
    guest_grads = guest_term(0, x["BM"])
    proj_grads += middle_term("C1")
    guest_grads += guest_term(1, x["C1M"])
    proj_grads, guest_grads = lax.optimization_barrier((proj_grads, guest_grads))
    proj_grads += middle_term("C2")
    guest_grads += guest_term(2, x["C2M"])
    proj_grads += middle_term("C3")
    proj_grads += near_term("C3", x["C3M"])
    proj_grads, guest_grads, masked = lax.optimization_barrier((proj_grads, guest_grads, masked))
    proj_grads += end_term("B")
    guest_grads += guest_term(3, x["BE"])
    proj_grads, guest_grads = lax.optimization_barrier((proj_grads, guest_grads))
    proj_grads += end_term("C1")
    guest_grads += guest_term(4, x["C1E"])
    guest_scores = lax.ppermute(column_scores(guest_acts.astype(jnp.float32), guest_grads, seq_count), "dp", TO_END) * scale[:, 0]

    proj_grads = after(proj_grads)
    proj_grads = after(proj_grads + end_term("C2"), guest_scores)
    proj_grads += end_term("C3")
    scores = rank_scores(column_scores(masked, proj_grads, seq_count) + guest_scores)
    other_scores = lax.ppermute(scores, "mp", [(0, 1), (1, 0)])
    return (scores + other_scores) / math.sqrt(RANK * LEN)


def suits_line(mesh, acts, left, right):
    unit = left.shape[0]
    fits = right.shape[0] * 2 == unit * 7 and acts.shape[0] * 2 == unit and left.shape[1] * 4 == unit
    return mesh.shape["dp"] == 4 and mesh.shape["mp"] == 2 and fits


def solution(mesh):
    def on_device(acts, grads, query_left, query_right, seq_len):
        body = on_line if suits_line(mesh, acts[0], query_left[0], query_right[0]) else on_any
        return body(acts[0], grads[0], query_left[0], query_right[0], seq_len)[None]

    return jax.shard_map(
        on_device,
        mesh=mesh,
        in_specs=(
            P("layer", ("groups", "dp"), "mp"),
            P("layer", ("groups", "dp"), "mp"),
            P("layer", ("mp", "dp"), "groups"),
            P("layer", ("mp", "dp"), "groups"),
            P(("groups", "dp")),
        ),
        out_specs=P("layer", ("groups", "dp"), None),
        check_vma=False,
    )
```

```python
import math

import jax
import jax.numpy as jnp
from jax import lax
from jax.sharding import PartitionSpec as P

RANK = 8
LEN = 256

TRADE = [(0, 1), (1, 0), (2, 3), (3, 2)]
TO_END = [(1, 0), (2, 3)]
ACROSS = [(1, 2), (2, 1)]
TO_MIDDLE = [(0, 1), (3, 2)]


def live_rows(seq_len, row_count):
    seq_count = seq_len.shape[0]
    seq_span = row_count // seq_count
    positions = lax.broadcasted_iota(jnp.int32, (seq_count, seq_span, 1), 1)
    live = (positions < seq_len[:, None, None]).astype(jnp.float32)
    return live.reshape(row_count, 1)


def column_scores(masked_acts, proj_grads, seq_count):
    product = masked_acts * proj_grads
    return jnp.sum(product.reshape(seq_count, -1, product.shape[1]), axis=1)


def rank_scores(columns):
    seq_count = columns.shape[0]
    return jnp.sum(columns.reshape(seq_count, -1, RANK), axis=2)


def dot(a, b):
    return jnp.dot(a, b, preferred_element_type=jnp.float32)


def on_any(acts, grads, left, right, seq_len):
    seq_count = seq_len.shape[0]
    live = live_rows(seq_len, acts.shape[0])
    proj_acts = dot(acts, lax.all_gather(left, "dp", axis=0, tiled=True))
    proj_grads = dot(grads, lax.all_gather(right, "dp", axis=0, tiled=True))
    masked = lax.psum(proj_acts, "mp") * live
    scores = rank_scores(column_scores(masked, proj_grads, seq_count))
    return lax.psum(scores, "mp") / math.sqrt(RANK * LEN)


def after(value, *arrived):
    return lax.optimization_barrier((value, *arrived))[0]


class Sender:
    def __init__(self, pairs):
        self.pairs = pairs
        self.came = []

    def ready(self, value, *arrived):
        return after(value, *self.came[-2:-1], *arrived)

    def __call__(self, x, pairs=None):
        self.came.append(lax.ppermute(x, "dp", pairs or self.pairs))
        return self.came[-1]


def on_line(acts, grads, left, right, seq_len):
    seq_count = seq_len.shape[0]
    row_count = acts.shape[0]
    place = lax.axis_index("dp")
    is_end = (place == 0) | (place == 3)
    near = place ^ 1
    far_middle = jnp.where(place < 2, 2, 1)
    far_end = jnp.where(place < 2, 3, 0)

    unit = left.shape[0]
    depth = right.shape[0]
    half = unit // 2
    spans = {"B": (0, unit), "C1": (unit, 2 * unit), "C2": (2 * unit, 3 * unit), "C3": (3 * unit, depth)}
    trade = Sender(TRADE)
    across = Sender(ACROSS)

    def columns(array, source, start, stop):
        span = array.shape[1] // 4
        return lax.dynamic_slice_in_dim(array, source * span + start, stop - start, axis=1)

    def own(name, sender):
        start, stop = spans[name]
        return sender.ready(right)[start:stop]

    def guest(index, sender):
        source = sender.ready(grads)
        start = unit + index * half
        middle = start + half // 2
        blocks = [columns(source, near, start, middle), columns(source, near, middle, start + half)]
        return jnp.concatenate(blocks, axis=0)

    def either(at_end, at_middle):
        return jnp.where(is_end, at_end, at_middle)

    x, y = {}, {}
    x["A"] = trade(left)
    y["AM"] = across(left)
    x["B"] = trade(right[:unit])
    y["AE"] = across(after(x["A"], y["AM"]))
    x["AM"] = trade(either(own("C1", trade), y["AM"]))
    y["BM"] = across(own("B", across))
    x["AE"] = trade(either(own("C2", trade), y["AE"]))
    y["C1M"] = across(own("C1", across))
    x["BM"] = trade(either(guest(0, trade), y["BM"]))
    y["C2M"] = across(own("C2", across))
    x["C1M"] = trade(either(guest(1, trade), y["C1M"]))
    y["C3M"] = across(own("C3", across))
    x["C2M"] = trade(either(guest(2, trade), y["C2M"]))
    y["BE"] = across(across.ready(x["B"]))
    x["C3M"] = trade(either(own("C3", trade), y["C3M"]))
    y["C1E"] = across(across.ready(x["AM"]))
    x["BE"] = trade(either(guest(3, trade), y["BE"]))
    y["C2E"] = across(across.ready(x["AE"]))
    x["C1E"] = trade(either(guest(4, trade), y["C1E"]))
    y["C3E"] = across(after(x["C3M"], y["C2E"]))
    x["C2E"] = trade(trade.ready(y["C2E"]), TO_END)
    x["C3E"] = trade(y["C3E"], TO_END)

    proj_acts = dot(columns(after(acts, x["A"], y["AM"]), place, 0, unit), left)
    proj_acts += dot(columns(acts, near, 0, unit), x["A"])
    proj_acts += dot(columns(acts, far_middle, 0, unit), either(x["AM"], y["AM"]))
    proj_acts += dot(columns(acts, far_end, 0, unit), either(x["AE"], y["AE"]))
    other_acts = lax.ppermute(proj_acts, "mp", [(0, 1), (1, 0)])
    masked = after((proj_acts + other_acts) * live_rows(seq_len, row_count))
    by_seq = masked.reshape(seq_count, -1, masked.shape[1])
    scale = jnp.maximum(jnp.max(jnp.abs(by_seq), axis=1, keepdims=True), 1e-30) / 32767
    coded = jnp.round(by_seq / scale).astype(jnp.int16).reshape(masked.shape)
    guest_acts = lax.ppermute(coded, "dp", TO_MIDDLE)

    def near_term(name, got):
        if name != "B":
            got = either(jnp.zeros_like(got), got)
        return dot(columns(grads, near, *spans[name]), got)

    def middle_term(name):
        return dot(columns(grads, far_middle, *spans[name]), either(x[name + "M"], y[name + "M"]))

    def end_term(name):
        return dot(columns(grads, far_end, *spans[name]), either(x[name + "E"], y[name + "E"]))

    def guest_term(index, got):
        start = unit + index * half
        terms = []
        for block in (0, 1):
            rows = got[block * row_count : (block + 1) * row_count]
            begin = start + block * (half // 2)
            terms.append(dot(rows, right[begin : begin + half // 2]))
        return terms[0] + terms[1]

    proj_grads = dot(columns(after(grads, x["AM"], y["AE"]), place, 0, depth), right)
    proj_grads = after(proj_grads, x["AE"])
    proj_grads += near_term("B", x["B"])
    proj_grads = after(proj_grads)
    proj_grads += near_term("C1", x["AM"])
    proj_grads += near_term("C2", x["AE"])
    proj_grads = after(proj_grads)
    proj_grads += middle_term("B")
    guest_grads = guest_term(0, x["BM"])
    proj_grads += middle_term("C1")
    guest_grads += guest_term(1, x["C1M"])
    proj_grads, guest_grads, coded = lax.optimization_barrier((proj_grads, guest_grads, coded))
    proj_grads += middle_term("C2")
    guest_grads += guest_term(2, x["C2M"])
    proj_grads += middle_term("C3")
    proj_grads += near_term("C3", x["C3M"])
    proj_grads, guest_grads, masked = lax.optimization_barrier((proj_grads, guest_grads, masked))
    proj_grads += end_term("B")
    guest_grads += guest_term(3, x["BE"])
    proj_grads, guest_grads = lax.optimization_barrier((proj_grads, guest_grads))
    proj_grads += end_term("C1")
    guest_grads += guest_term(4, x["C1E"])
    guest_scores = lax.ppermute(column_scores(guest_acts.astype(jnp.float32), guest_grads, seq_count), "dp", TO_END) * scale[:, 0]

    proj_grads = after(proj_grads)
    proj_grads = after(proj_grads + end_term("C2"), guest_scores)
    proj_grads += end_term("C3")
    scores = rank_scores(column_scores(masked, proj_grads, seq_count) + guest_scores)
    other_scores = lax.ppermute(scores, "mp", [(0, 1), (1, 0)])
    return (scores + other_scores) / math.sqrt(RANK * LEN)


def suits_line(mesh, acts, left, right):
    unit = left.shape[0]
    fits = right.shape[0] * 2 == unit * 7 and acts.shape[0] * 2 == unit and left.shape[1] * 4 == unit
    return mesh.shape["dp"] == 4 and mesh.shape["mp"] == 2 and fits


def solution(mesh):
    def on_device(acts, grads, query_left, query_right, seq_len):
        body = on_line if suits_line(mesh, acts[0], query_left[0], query_right[0]) else on_any
        return body(acts[0], grads[0], query_left[0], query_right[0], seq_len)[None]

    return jax.shard_map(
        on_device,
        mesh=mesh,
        in_specs=(
            P("layer", ("groups", "dp"), "mp"),
            P("layer", ("groups", "dp"), "mp"),
            P("layer", ("mp", "dp"), "groups"),
            P("layer", ("mp", "dp"), "groups"),
            P(("groups", "dp")),
        ),
        out_specs=P("layer", ("groups", "dp"), None),
        check_vma=False,
    )
```

```python
import math

import jax
import jax.numpy as jnp
from jax import lax
from jax.sharding import PartitionSpec as P

RANK = 8
LEN = 256

TRADE = [(0, 1), (1, 0), (2, 3), (3, 2)]
TO_END = [(1, 0), (2, 3)]
ACROSS = [(1, 2), (2, 1)]
TO_MIDDLE = [(0, 1), (3, 2)]


def live_rows(seq_len, row_count):
    seq_count = seq_len.shape[0]
    seq_span = row_count // seq_count
    positions = lax.broadcasted_iota(jnp.int32, (seq_count, seq_span, 1), 1)
    live = (positions < seq_len[:, None, None]).astype(jnp.float32)
    return live.reshape(row_count, 1)


def column_scores(masked_acts, proj_grads, seq_count):
    product = masked_acts * proj_grads
    return jnp.sum(product.reshape(seq_count, -1, product.shape[1]), axis=1)


def rank_scores(columns):
    seq_count = columns.shape[0]
    return jnp.sum(columns.reshape(seq_count, -1, RANK), axis=2)


def dot(a, b):
    return jnp.dot(a, b, preferred_element_type=jnp.float32)


def on_any(acts, grads, left, right, seq_len):
    seq_count = seq_len.shape[0]
    live = live_rows(seq_len, acts.shape[0])
    proj_acts = dot(acts, lax.all_gather(left, "dp", axis=0, tiled=True))
    proj_grads = dot(grads, lax.all_gather(right, "dp", axis=0, tiled=True))
    masked = lax.psum(proj_acts, "mp") * live
    scores = rank_scores(column_scores(masked, proj_grads, seq_count))
    return lax.psum(scores, "mp") / math.sqrt(RANK * LEN)


def after(value, *arrived):
    return lax.optimization_barrier((value, *arrived))[0]


class Sender:
    def __init__(self, pairs):
        self.pairs = pairs
        self.came = []

    def ready(self, value, *arrived):
        return after(value, *self.came[-2:-1], *arrived)

    def __call__(self, x, pairs=None):
        self.came.append(lax.ppermute(x, "dp", pairs or self.pairs))
        return self.came[-1]


def on_line(acts, grads, left, right, seq_len):
    seq_count = seq_len.shape[0]
    row_count = acts.shape[0]
    place = lax.axis_index("dp")
    is_end = (place == 0) | (place == 3)
    near = place ^ 1
    far_middle = jnp.where(place < 2, 2, 1)
    far_end = jnp.where(place < 2, 3, 0)

    unit = left.shape[0]
    depth = right.shape[0]
    half = unit // 2
    spans = {"B": (0, unit), "C1": (unit, 2 * unit), "C2": (2 * unit, 3 * unit), "C3": (3 * unit, depth)}
    trade = Sender(TRADE)
    across = Sender(ACROSS)

    def columns(array, source, start, stop):
        span = array.shape[1] // 4
        return lax.dynamic_slice_in_dim(array, source * span + start, stop - start, axis=1)

    def own(name, sender):
        start, stop = spans[name]
        return sender.ready(right)[start:stop]

    def guest(index, sender):
        source = sender.ready(grads)
        start = unit + index * half
        middle = start + half // 2
        blocks = [columns(source, near, start, middle), columns(source, near, middle, start + half)]
        return jnp.concatenate(blocks, axis=0)

    def either(at_end, at_middle):
        return jnp.where(is_end, at_end, at_middle)

    x, y = {}, {}
    x["A"] = trade(left)
    y["AM"] = across(left)
    x["B"] = trade(right[:unit])
    y["AE"] = across(after(x["A"], y["AM"]))
    x["AM"] = trade(either(own("C1", trade), y["AM"]))
    y["BM"] = across(own("B", across))
    x["AE"] = trade(either(own("C2", trade), y["AE"]))
    y["C1M"] = across(own("C1", across))
    x["BM"] = trade(either(guest(0, trade), y["BM"]))
    y["C2M"] = across(own("C2", across))
    x["C1M"] = trade(either(guest(1, trade), y["C1M"]))
    y["C3M"] = across(own("C3", across))
    x["C2M"] = trade(either(guest(2, trade), y["C2M"]))
    y["BE"] = across(across.ready(x["B"]))
    x["C3M"] = trade(either(own("C3", trade), y["C3M"]))
    y["C1E"] = across(across.ready(x["AM"]))
    x["BE"] = trade(either(guest(3, trade), y["BE"]))
    y["C2E"] = across(across.ready(x["AE"]))
    x["C1E"] = trade(either(guest(4, trade), y["C1E"]))
    y["C3E"] = across(after(x["C3M"], y["C2E"]))
    x["C2E"] = trade(trade.ready(y["C2E"]), TO_END)
    x["C3E"] = trade(y["C3E"], TO_END)

    x["C1E"] = after(x["C1E"], y["C3E"])

    proj_acts = dot(columns(after(acts, x["A"], y["AM"]), place, 0, unit), left)
    proj_acts += dot(columns(acts, near, 0, unit), x["A"])
    proj_acts += dot(columns(acts, far_middle, 0, unit), either(x["AM"], y["AM"]))
    proj_acts += dot(columns(acts, far_end, 0, unit), either(x["AE"], y["AE"]))
    other_acts = lax.ppermute(proj_acts, "mp", [(0, 1), (1, 0)])
    masked = after((proj_acts + other_acts) * live_rows(seq_len, row_count))
    by_seq = masked.reshape(seq_count, -1, masked.shape[1])
    scale = jnp.maximum(jnp.max(jnp.abs(by_seq), axis=1, keepdims=True), 1e-30) / 32767
    coded = jnp.round(by_seq / scale).astype(jnp.int16).reshape(masked.shape)
    guest_acts = lax.ppermute(coded, "dp", TO_MIDDLE)

    def near_term(name, got):
        if name != "B":
            got = either(jnp.zeros_like(got), got)
        return dot(columns(grads, near, *spans[name]), got)

    def middle_term(name):
        return dot(columns(grads, far_middle, *spans[name]), either(x[name + "M"], y[name + "M"]))

    def end_term(name):
        return dot(columns(grads, far_end, *spans[name]), either(x[name + "E"], y[name + "E"]))

    def guest_term(index, got):
        start = unit + index * half
        terms = []
        for block in (0, 1):
            rows = got[block * row_count : (block + 1) * row_count]
            begin = start + block * (half // 2)
            terms.append(dot(rows, right[begin : begin + half // 2]))
        return terms[0] + terms[1]

    proj_grads = dot(columns(after(grads, x["AM"], y["AE"]), place, 0, depth), right)
    proj_grads = after(proj_grads, x["AE"])
    proj_grads += near_term("B", x["B"])
    proj_grads = after(proj_grads)
    proj_grads += near_term("C1", x["AM"])
    proj_grads += near_term("C2", x["AE"])
    proj_grads = after(proj_grads)
    proj_grads += middle_term("B")
    guest_grads = guest_term(0, x["BM"])
    proj_grads += middle_term("C1")
    guest_grads += guest_term(1, x["C1M"])
    proj_grads, guest_grads, coded = lax.optimization_barrier((proj_grads, guest_grads, coded))
    proj_grads += middle_term("C2")
    guest_grads += guest_term(2, x["C2M"])
    proj_grads += middle_term("C3")
    proj_grads += near_term("C3", x["C3M"])
    proj_grads, guest_grads, masked = lax.optimization_barrier((proj_grads, guest_grads, masked))
    proj_grads += end_term("B")
    guest_grads += guest_term(3, x["BE"])
    proj_grads, guest_grads = lax.optimization_barrier((proj_grads, guest_grads))
    proj_grads += end_term("C1")
    guest_grads += guest_term(4, x["C1E"])
    guest_scores = lax.ppermute(column_scores(guest_acts.astype(jnp.float32), guest_grads, seq_count), "dp", TO_END) * scale[:, 0]

    proj_grads = after(proj_grads)
    proj_grads = after(proj_grads + end_term("C2"), guest_scores)
    proj_grads += end_term("C3")
    scores = rank_scores(column_scores(masked, proj_grads, seq_count) + guest_scores)
    other_scores = lax.ppermute(scores, "mp", [(0, 1), (1, 0)])
    return (scores + other_scores) / math.sqrt(RANK * LEN)


def suits_line(mesh, acts, left, right):
    unit = left.shape[0]
    fits = right.shape[0] * 2 == unit * 7 and acts.shape[0] * 2 == unit and left.shape[1] * 4 == unit
    return mesh.shape["dp"] == 4 and mesh.shape["mp"] == 2 and fits


def solution(mesh):
    def on_device(acts, grads, query_left, query_right, seq_len):
        body = on_line if suits_line(mesh, acts[0], query_left[0], query_right[0]) else on_any
        return body(acts[0], grads[0], query_left[0], query_right[0], seq_len)[None]

    return jax.shard_map(
        on_device,
        mesh=mesh,
        in_specs=(
            P("layer", ("groups", "dp"), "mp"),
            P("layer", ("groups", "dp"), "mp"),
            P("layer", ("mp", "dp"), "groups"),
            P("layer", ("mp", "dp"), "groups"),
            P(("groups", "dp")),
        ),
        out_specs=P("layer", ("groups", "dp"), None),
        check_vma=False,
    )
```

```python
import math

import jax
import jax.numpy as jnp
from jax import lax
from jax.sharding import PartitionSpec as P

RANK = 8
LEN = 256

TRADE = [(0, 1), (1, 0), (2, 3), (3, 2)]
TO_END = [(1, 0), (2, 3)]
ACROSS = [(1, 2), (2, 1)]
TO_MIDDLE = [(0, 1), (3, 2)]


def live_rows(seq_len, row_count):
    seq_count = seq_len.shape[0]
    seq_span = row_count // seq_count
    positions = lax.broadcasted_iota(jnp.int32, (seq_count, seq_span, 1), 1)
    live = (positions < seq_len[:, None, None]).astype(jnp.float32)
    return live.reshape(row_count, 1)


def column_scores(masked_acts, proj_grads, seq_count):
    product = masked_acts * proj_grads
    return jnp.sum(product.reshape(seq_count, -1, product.shape[1]), axis=1)


def rank_scores(columns):
    seq_count = columns.shape[0]
    return jnp.sum(columns.reshape(seq_count, -1, RANK), axis=2)


def dot(a, b):
    return jnp.dot(a, b, preferred_element_type=jnp.float32)


def on_any(acts, grads, left, right, seq_len):
    seq_count = seq_len.shape[0]
    live = live_rows(seq_len, acts.shape[0])
    proj_acts = dot(acts, lax.all_gather(left, "dp", axis=0, tiled=True))
    proj_grads = dot(grads, lax.all_gather(right, "dp", axis=0, tiled=True))
    masked = lax.psum(proj_acts, "mp") * live
    scores = rank_scores(column_scores(masked, proj_grads, seq_count))
    return lax.psum(scores, "mp") / math.sqrt(RANK * LEN)


def after(value, *arrived):
    return lax.optimization_barrier((value, *arrived))[0]


class Sender:
    def __init__(self, pairs):
        self.pairs = pairs
        self.came = []

    def ready(self, value, *arrived):
        return after(value, *self.came[-2:-1], *arrived)

    def __call__(self, x, pairs=None):
        self.came.append(lax.ppermute(x, "dp", pairs or self.pairs))
        return self.came[-1]


def on_line(acts, grads, left, right, seq_len):
    seq_count = seq_len.shape[0]
    row_count = acts.shape[0]
    place = lax.axis_index("dp")
    is_end = (place == 0) | (place == 3)
    near = place ^ 1
    far_middle = jnp.where(place < 2, 2, 1)
    far_end = jnp.where(place < 2, 3, 0)

    unit = left.shape[0]
    depth = right.shape[0]
    half = unit // 2
    spans = {"B": (0, unit), "C1": (unit, 2 * unit), "C2": (2 * unit, 3 * unit), "C3": (3 * unit, depth)}
    trade = Sender(TRADE)
    across = Sender(ACROSS)

    def columns(array, source, start, stop):
        span = array.shape[1] // 4
        return lax.dynamic_slice_in_dim(array, source * span + start, stop - start, axis=1)

    def own(name, sender):
        start, stop = spans[name]
        return sender.ready(right)[start:stop]

    def guest(index, sender):
        source = sender.ready(grads)
        start = unit + index * half
        middle = start + half // 2
        blocks = [columns(source, near, start, middle), columns(source, near, middle, start + half)]
        return jnp.concatenate(blocks, axis=0)

    def either(at_end, at_middle):
        return jnp.where(is_end, at_end, at_middle)

    x, y = {}, {}
    x["A"] = trade(left)
    y["AM"] = across(left)
    x["B"] = trade(right[:unit])
    y["AE"] = across(after(x["A"], y["AM"]))
    x["AM"] = trade(either(own("C1", trade), y["AM"]))
    y["BM"] = across(own("B", across))
    x["AE"] = trade(either(own("C2", trade), y["AE"]))
    y["C1M"] = across(own("C1", across))
    x["BM"] = trade(either(guest(0, trade), y["BM"]))
    y["C2M"] = across(own("C2", across))
    x["C1M"] = trade(either(guest(1, trade), y["C1M"]))
    y["C3M"] = across(own("C3", across))
    x["C2M"] = trade(either(guest(2, trade), y["C2M"]))
    y["BE"] = across(after(x["B"], y["C1M"]))
    x["C3M"] = trade(either(own("C3", trade), y["C3M"]))
    y["C1E"] = across(across.ready(x["AM"]))
    x["BE"] = trade(either(guest(3, trade), y["BE"]))
    y["C2E"] = across(across.ready(x["AE"]))
    x["C1E"] = trade(either(guest(4, trade), y["C1E"]))
    y["C3E"] = across(after(x["C3M"], y["C2E"]))
    x["C2E"] = trade(trade.ready(y["C2E"]), TO_END)
    x["C3E"] = trade(y["C3E"], TO_END)

    proj_acts = dot(columns(after(acts, x["A"], y["AM"]), place, 0, unit), left)
    proj_acts += dot(columns(acts, near, 0, unit), x["A"])
    proj_acts += dot(columns(acts, far_middle, 0, unit), either(x["AM"], y["AM"]))
    proj_acts += dot(columns(acts, far_end, 0, unit), either(x["AE"], y["AE"]))
    other_acts = lax.ppermute(proj_acts, "mp", [(0, 1), (1, 0)])
    masked = after((proj_acts + other_acts) * live_rows(seq_len, row_count))
    by_seq = masked.reshape(seq_count, -1, masked.shape[1])
    scale = jnp.maximum(jnp.max(jnp.abs(by_seq), axis=1, keepdims=True), 1e-30) / 32767
    coded = jnp.round(by_seq / scale).astype(jnp.int16).reshape(masked.shape)
    guest_acts = lax.ppermute(coded, "dp", TO_MIDDLE)

    def near_term(name, got):
        if name != "B":
            got = either(jnp.zeros_like(got), got)
        return dot(columns(grads, near, *spans[name]), got)

    def middle_term(name):
        return dot(columns(grads, far_middle, *spans[name]), either(x[name + "M"], y[name + "M"]))

    def end_term(name):
        return dot(columns(grads, far_end, *spans[name]), either(x[name + "E"], y[name + "E"]))

    def guest_term(index, got):
        start = unit + index * half
        terms = []
        for block in (0, 1):
            rows = got[block * row_count : (block + 1) * row_count]
            begin = start + block * (half // 2)
            terms.append(dot(rows, right[begin : begin + half // 2]))
        return terms[0] + terms[1]

    proj_grads = dot(columns(after(grads, x["AM"], y["AE"]), place, 0, depth), right)
    proj_grads = after(proj_grads, x["AE"])
    proj_grads += near_term("B", x["B"])
    proj_grads = after(proj_grads)
    proj_grads += near_term("C1", x["AM"])
    proj_grads += near_term("C2", x["AE"])
    proj_grads = after(proj_grads)
    proj_grads += middle_term("B")
    guest_grads = guest_term(0, x["BM"])
    proj_grads += middle_term("C1")
    guest_grads += guest_term(1, x["C1M"])
    proj_grads, guest_grads = lax.optimization_barrier((proj_grads, guest_grads))
    proj_grads += middle_term("C2")
    guest_grads += guest_term(2, x["C2M"])
    proj_grads += middle_term("C3")
    proj_grads += near_term("C3", x["C3M"])
    proj_grads, guest_grads, masked = lax.optimization_barrier((proj_grads, guest_grads, masked))
    proj_grads += end_term("B")
    guest_grads += guest_term(3, x["BE"])
    proj_grads, guest_grads = lax.optimization_barrier((proj_grads, guest_grads))
    proj_grads += end_term("C1")
    guest_grads += guest_term(4, x["C1E"])
    guest_scores = lax.ppermute(column_scores(guest_acts.astype(jnp.float32), guest_grads, seq_count), "dp", TO_END) * scale[:, 0]

    proj_grads = after(proj_grads)
    proj_grads = after(proj_grads + end_term("C2"), guest_scores)
    proj_grads += end_term("C3")
    scores = rank_scores(column_scores(masked, proj_grads, seq_count) + guest_scores)
    other_scores = lax.ppermute(scores, "mp", [(0, 1), (1, 0)])
    return (scores + other_scores) / math.sqrt(RANK * LEN)


def suits_line(mesh, acts, left, right):
    unit = left.shape[0]
    fits = right.shape[0] * 2 == unit * 7 and acts.shape[0] * 2 == unit and left.shape[1] * 4 == unit
    return mesh.shape["dp"] == 4 and mesh.shape["mp"] == 2 and fits


def solution(mesh):
    def on_device(acts, grads, query_left, query_right, seq_len):
        body = on_line if suits_line(mesh, acts[0], query_left[0], query_right[0]) else on_any
        return body(acts[0], grads[0], query_left[0], query_right[0], seq_len)[None]

    return jax.shard_map(
        on_device,
        mesh=mesh,
        in_specs=(
            P("layer", ("groups", "dp"), "mp"),
            P("layer", ("groups", "dp"), "mp"),
            P("layer", ("mp", "dp"), "groups"),
            P("layer", ("mp", "dp"), "groups"),
            P(("groups", "dp")),
        ),
        out_specs=P("layer", ("groups", "dp"), None),
        check_vma=False,
    )
```
